256 devices in a mesh: group: 16 (over z, y_hi), node: 16 (over x, y_lo, core).
Axes of the slice: x: 4, y: 4 (y_hi: 2, y_lo: 2; y = y_hi * 2 + y_lo), z: 8, core: 2. Of those that a mesh axis runs over, the one named last changes fastest.
Arguments:
- grads: bfloat16 [256, 4194304], P(('group', 'node')), may hold values from -24 to 24
- master: float32 [4194304], P(('group', 'node')), may hold values from -6 to 6
- moment: float32 [4194304], P(('group', 'node')), may hold values from -6 to 6
- second: float32 [4194304], P(('group', 'node')), may hold values from 1 to 400
Outputs:
- master_out: float32 [4194304], P(('group', 'node'))
- moment_out: float32 [4194304], P(('group', 'node'))
- second_out: float32 [4194304], P(('group', 'node'))
The draws below stay inside these ranges and needn't reach their ends.
All inputs are finite; a program needn't handle non-finite values.
Results may differ from the reference program's by a relative error of at most 0.0012.
Values may be sent and summed in bfloat16 or wider, within the bound.
No kernel may reach another device: no remote copies, remote signals or barrier semaphores. Data moves between devices by JAX's collectives and lax.ppermute only.
A program may use at most 128 MiB of HBM per device.

```python
import math
import jax
import jax.numpy as jnp
from jax import lax

BLOCK = 512
PARAMS = 4194304
N_GROUP = 16
N_NODE = 16
DEVICES = 256


def raised(drawn, rng, source, target, parts, factor):
    def block_of(axis_at):
        return (jnp.arange(drawn.shape[axis_at]) // (drawn.shape[axis_at] // parts)).reshape((-1,) + (1,) * (drawn.ndim - 1 - axis_at))

    near = jax.random.permutation(rng, parts)[block_of(target)]
    far = (block_of(target) + parts // 2) % parts
    return jnp.where((block_of(source) == near) | (block_of(source) == far), factor * drawn, drawn)


def steps_of(own_key, extent, pieces, low, top_value):
    level = 1.0
    for axis_at, blocks in pieces:
        heights = jax.random.uniform(jax.random.fold_in(jax.random.fold_in(own_key, 6), axis_at), (blocks,), jnp.float32, low / len(pieces), top_value / len(pieces))
        level = level * jnp.repeat(jnp.exp(heights), extent[axis_at] // blocks).reshape((-1,) + (1,) * (len(extent) - 1 - axis_at))
    return level


def scatter_about(rng, extent, width, bound, pieces=(), held_as=jnp.bfloat16):
    drawn = jax.random.normal(rng, extent, jnp.float32) * width
    if len(pieces) > 0:
        drawn = steps_of(rng, extent, pieces, -0.22, 0.18) * drawn
    return jnp.clip(drawn, min=-bound, max=bound).astype(held_as)


def noise_with(own_key, shape, scale, most, split, heavy, held_as=jnp.bfloat16):
    values = scale * jax.random.normal(own_key, shape, jnp.float32)
    if split:
        values = values * steps_of(own_key, shape, split, -0.22, 0.18)
    return jnp.clip(raised(values, jax.random.fold_in(own_key, 3), *heavy), -most, most).astype(held_as)


def setup_inputs(seed: int = 0) -> dict:
    keys = jax.random.split(jax.random.key(seed), 5)
    return {
        "grads": noise_with(keys[0], (DEVICES, PARAMS), 1.0, 24.0, ((0, 256),), (0, 1, 256, 6.0)),
        "master": scatter_about(keys[1], (PARAMS,), 1.0, 6.0, ((0, 256),), jnp.float32),
        "moment": scatter_about(keys[2], (PARAMS,), 1.0, 6.0, ((0, 256),), jnp.float32),
        "second": jnp.clip(jnp.exp(math.log(400.0) - 5.9914645 * jax.random.uniform(keys[3], (PARAMS,), jnp.float32) ** steps_of(keys[3], (PARAMS,), ((0, 256),), -0.2, 0.2)), 1.0, 400.0),
    }


def quantize(values):
    block_peak = lax.optimization_barrier(jnp.max(jnp.abs(values), axis=-1))
    scales = jnp.full(block_peak.shape, 2.0 ** (-24), jnp.float32)
    for exponent in range(-24, 17):
        scales = jnp.where(block_peak > 127.0 * 2.0 ** exponent, jnp.float32(2.0 ** (exponent + 1)), scales)
    codes = jnp.floor(values / scales[..., None] + 0.5).astype(jnp.bfloat16)
    return (codes, scales)

def dequantize(codes, scales):
    return codes.astype(jnp.float32) * scales.astype(jnp.float32)[..., None]

def reference(grads, master, moment, second):
    block_count = PARAMS // BLOCK
    shaped = grads.reshape(N_GROUP, N_NODE, block_count, BLOCK)

    def per_group(members):
        codes, scales = quantize(members.astype(jnp.float32))
        partial_value = lax.optimization_barrier(jnp.sum(dequantize(codes, scales), axis=0))
        return quantize(partial_value)
    second_quant, second_scale = lax.map(per_group, shaped)
    gradient = lax.optimization_barrier(jnp.sum(dequantize(second_quant, second_scale), axis=0)).reshape(PARAMS)
    moment_out = 0.9 * moment + 0.1 * gradient
    second_out = 0.95 * second + 0.05 * gradient * gradient
    master_out = master - 0.02 * (moment_out / (jnp.sqrt(second_out) + 1e-08) + 0.1 * master)
    return (master_out, moment_out, second_out)
```

```python
import jax
import jax.numpy as jnp
from jax import lax
from jax.experimental import pallas as pl
from jax.experimental.pallas import tpu as pltpu
from jax.sharding import PartitionSpec as P

BLOCK = 512
LANES = 128
ROWS = BLOCK // LANES
GROUP_ROWS = 8 * ROWS
GROUP = GROUP_ROWS * LANES


def scale_of(peak):
    scale = jnp.full(peak.shape, 2.0**-24, jnp.float32)
    inverse = jnp.full(peak.shape, 2.0**24, jnp.float32)
    for k in (16, 8, 4, 2, 1):
        above = peak > scale * (127.0 * 2.0 ** (k - 1))
        scale = jnp.where(above, scale * 2.0**k, scale)
        inverse = jnp.where(above, inverse * 2.0**-k, inverse)
    return scale, inverse


def requantized(parts):
    peak = jnp.abs(parts[0])
    for part in parts[1:]:
        peak = jnp.maximum(peak, jnp.abs(part))
    peak = jnp.max(peak, axis=1, keepdims=True)
    scale, inverse = scale_of(jnp.broadcast_to(peak, parts[0].shape))
    return [jnp.floor(part * inverse + 0.5) * scale for part in parts]


def first_kernel(nodes, groups, x_ref, o_ref, scratch):
    def step(n, carry):
        for k in range(groups):
            at = pl.multiple_of((n * groups + k) * GROUP, GROUP)
            scratch[k] = x_ref[0:1, pl.ds(at, GROUP)].astype(jnp.float32).reshape(GROUP_ROWS, LANES)
        for k in range(groups):
            parts = [scratch[k, pl.ds(s, 8, stride=ROWS), :] for s in range(ROWS)]
            done = jnp.concatenate(requantized(parts), axis=0)
            o_ref[n, 0, k * GROUP_ROWS : (k + 1) * GROUP_ROWS, :] = done.astype(jnp.bfloat16)
        return carry

    lax.fori_loop(0, nodes, step, 0, unroll=2)


def second_kernel(nodes, groups, r_ref, o_ref):
    for k in range(groups):
        rows = slice(k * GROUP_ROWS, (k + 1) * GROUP_ROWS)
        total = r_ref[0, 0, rows, :].astype(jnp.float32)
        for n in range(1, nodes):
            total = total + r_ref[n, 0, rows, :].astype(jnp.float32)
        parts = [total[8 * s : 8 * s + 8] for s in range(ROWS)]
        done = jnp.concatenate(requantized(parts), axis=0)
        o_ref[0, rows, :] = done.astype(jnp.bfloat16)


def update_kernel(replicas, groups, r_ref, p_ref, m_ref, v_ref, po_ref, mo_ref, vo_ref, scratch):
    for k in range(groups):
        rows = slice(k * GROUP_ROWS, (k + 1) * GROUP_ROWS)
        total = r_ref[0, rows, :].astype(jnp.float32)
        for g in range(1, replicas):
            total = total + r_ref[g, rows, :].astype(jnp.float32)
        for s in range(ROWS):
            scratch[pl.ds(k * GROUP_ROWS + s, 8, stride=ROWS), :] = total[8 * s : 8 * s + 8]
    gradient = scratch[...]
    master = p_ref[...]
    moment = 0.9 * m_ref[...] + 0.1 * gradient
    second = 0.95 * v_ref[...] + 0.05 * gradient * gradient
    mo_ref[...] = moment
    vo_ref[...] = second
    po_ref[...] = master - 0.02 * (moment / (jnp.sqrt(second) + 1e-08) + 0.1 * master)


def body(grads, master, moment, second):
    replicas = lax.axis_size("group")
    nodes = lax.axis_size("node")
    shard = master.shape[0]
    rows = shard // LANES
    groups = shard // GROUP
    params = pltpu.CompilerParams(vmem_limit_bytes=32 << 20)
    first = pl.pallas_call(
        lambda *refs: first_kernel(nodes, groups, *refs),
        name="first_quantize",
        grid=(replicas,),
        in_specs=[pl.BlockSpec((1, nodes * shard), lambda g: (0, g))],
        out_specs=pl.BlockSpec((nodes, 1, rows, LANES), lambda g: (0, g, 0, 0)),
        out_shape=jax.ShapeDtypeStruct((nodes, replicas, rows, LANES), jnp.bfloat16),
        scratch_shapes=[pltpu.VMEM((groups, GROUP_ROWS, LANES), jnp.float32)],
        compiler_params=params,
    )(grads)
    received = lax.all_to_all(first, "node", split_axis=0, concat_axis=0, tiled=True)
    partial = pl.pallas_call(
        lambda *refs: second_kernel(nodes, groups, *refs),
        name="sum_and_requantize",
        grid=(replicas,),
        in_specs=[pl.BlockSpec((nodes, 1, rows, LANES), lambda g: (0, g, 0, 0))],
        out_specs=pl.BlockSpec((1, rows, LANES), lambda g: (g, 0, 0)),
        out_shape=jax.ShapeDtypeStruct((replicas, rows, LANES), jnp.bfloat16),
        compiler_params=params,
    )(received)
    owned = lax.all_to_all(partial, "group", split_axis=0, concat_axis=0, tiled=True)
    state = jax.ShapeDtypeStruct((rows, LANES), jnp.float32)
    outs = pl.pallas_call(
        lambda *refs: update_kernel(replicas, groups, *refs),
        name="adamw_update",
        out_shape=(state, state, state),
        scratch_shapes=[pltpu.VMEM((rows, LANES), jnp.float32)],
        compiler_params=params,
    )(owned, *(a.reshape(rows, LANES) for a in (master, moment, second)))
    return tuple(a.reshape(shard) for a in outs)


def solution(mesh):
    split = P(("group", "node"))
    in_specs = (P(("group", "node"), None), split, split, split)
    return jax.shard_map(
        body, mesh=mesh, in_specs=in_specs, out_specs=(split, split, split), check_vma=False
    )
```

```python
import jax
import jax.numpy as jnp
from jax import lax
from jax.experimental import pallas as pl
from jax.experimental.pallas import tpu as pltpu
from jax.sharding import Mesh
from jax.sharding import PartitionSpec as P

BLOCK = 512
LANES = 128
ROWS = BLOCK // LANES
GROUP_ROWS = 8 * ROWS
GROUP = GROUP_ROWS * LANES
SEND_LANE = 64
AUX_ROWS = 16

RATIO = 64.0
STEPS = 72.0
OFFSET = 113.0

PARTS = (3, 5, 8)
PARAMS = pltpu.CompilerParams(vmem_limit_bytes=48 << 20)


def scale_of(peak):
    scale = jnp.full(peak.shape, 2.0**-24, jnp.float32)
    inverse = jnp.full(peak.shape, 2.0**24, jnp.float32)
    for k in (16, 8, 4, 2, 1):
        above = peak > scale * (127.0 * 2.0 ** (k - 1))
        scale = jnp.where(above, scale * 2.0**k, scale)
        inverse = jnp.where(above, inverse * 2.0**-k, inverse)
    return scale, inverse


def peak_of(parts):
    peak = jnp.abs(parts[0])
    for part in parts[1:]:
        peak = jnp.maximum(peak, jnp.abs(part))
    return jnp.max(peak, axis=1, keepdims=True)


def requantized(parts):
    scale, inverse = scale_of(jnp.broadcast_to(peak_of(parts), parts[0].shape))
    return [jnp.floor(part * inverse + 0.5) * scale for part in parts]


def pair_kernel(chips, groups, core_ref, x_ref, after_ref, own_ref, send_ref, scale_ref, scratch):
    del after_ref
    core = core_ref[0]
    lane = lax.broadcasted_iota(jnp.int32, (8, LANES), 1)
    where = [(d, half, k) for d in range(chips) for half in range(2) for k in range(groups)]

    for d, half, k in where:
        node = 2 * d + (core if half == 0 else 1 - core)
        at = pl.multiple_of((node * groups + k) * GROUP, GROUP)
        rows = x_ref[0:1, pl.ds(at, GROUP)].astype(jnp.float32).reshape(GROUP_ROWS, LANES)
        scratch[d, half * groups + k] = rows

    def parts_of(d, half, k):
        return [scratch[d, half * groups + k, pl.ds(s, 8, stride=ROWS), :] for s in range(ROWS)]

    tiles = [jnp.zeros((8, LANES), jnp.float32)] * groups
    for d, half, k in where:
        column = lane == half * SEND_LANE + d * groups + k
        tiles[k] = jnp.where(column, peak_of(parts_of(d, half, k)), tiles[k])
    tile = tiles[0]
    for k in range(1, groups):
        tile = jnp.maximum(tile, tiles[k])
    scale, inverse = scale_of(tile)
    scale_ref[0] = jnp.where(tile > 0, scale, 0.0)

    for d, half, k in where:
        at = half * SEND_LANE + d * groups + k
        s_col = jnp.broadcast_to(scale[:, at : at + 1], (8, LANES))
        i_col = jnp.broadcast_to(inverse[:, at : at + 1], (8, LANES))
        done = [jnp.floor(part * i_col + 0.5) * s_col for part in parts_of(d, half, k)]
        o_ref = send_ref if half else own_ref
        at = slice(k * GROUP_ROWS, (k + 1) * GROUP_ROWS)
        o_ref[d, 0, at, :] = jnp.concatenate(done, axis=0).astype(jnp.bfloat16)


def encode_kernel(
    chips, groups, count, own_ref, peer_ref, mine_ref, theirs_ref, before_ref, m_ref, flag_ref,
    buffer, aux, packed, bad, sems, aux_sem,
):
    g = pl.program_id(0)
    slot = lax.rem(g, 2)
    rows = groups * GROUP_ROWS
    lane = lax.broadcasted_iota(jnp.int32, (8, LANES), 1)

    def copy(step, at):
        where = m_ref.at[:, pl.ds(pl.multiple_of(step * rows, rows), rows), :]
        return pltpu.make_async_copy(buffer.at[at], where, sems.at[at])

    @pl.when(g == 0)
    def _():
        bad[...] = before_ref[...]
        packed[...] = jnp.ones_like(packed)

    @pl.when(g >= 2)
    def _():
        copy(g - 2, slot).wait()

    mine, theirs = mine_ref[0], pltpu.roll(theirs_ref[0], SEND_LANE, 1)
    high, low = jnp.maximum(mine, theirs), jnp.minimum(mine, theirs)
    bad[...] = jnp.where((low > 0) & (high > RATIO * low), 1.0, bad[...])
    scale, inverse = scale_of(127.0 * high)
    weight = inverse * (RATIO / STEPS)

    for d in range(chips):
        tile = packed[d]
        for k in range(groups):
            column = slice(d * groups + k, d * groups + k + 1)
            tile = jnp.where(lane == g * groups + k, scale[:, column], tile)
            w_col = jnp.broadcast_to(weight[:, column], (8, LANES))
            at = slice(k * GROUP_ROWS, (k + 1) * GROUP_ROWS)
            total = own_ref[d, 0, at, :].astype(jnp.float32) + peer_ref[d, 0, at, :].astype(jnp.float32)
            out = []
            for s in range(ROWS):
                part = total[8 * s : 8 * s + 8]
                code = jnp.exp2(jnp.abs(part) * w_col - OFFSET)
                out.append(jnp.where(part < 0, -code, code))
            buffer[slot, d, at, :] = jnp.concatenate(out, axis=0).astype(jnp.bfloat16)
        packed[d] = tile
    copy(g, slot).start()

    @pl.when(g == count - 1)
    def _():
        flag = jnp.max(bad[...])
        flag_ref[...] = bad[...]
        for d in range(chips):
            unit = packed[d] * jnp.where(flag > 0, jnp.float32(jnp.nan), 1.0 / RATIO)
            aux[d] = jnp.concatenate([unit, unit], axis=0).astype(jnp.bfloat16)
        last = pltpu.make_async_copy(aux, m_ref.at[:, pl.ds(count * rows, AUX_ROWS), :], aux_sem)
        last.start()
        last.wait()
        if count >= 2:
            copy(g - 1, 1 - slot).wait()
        copy(g, slot).wait()


def decode_kernel(chips, groups, r_ref, aux_ref, o_ref, units):
    g = pl.program_id(0)

    @pl.when(g == 0)
    def _():
        for d in range(chips):
            units[d] = aux_ref[d].astype(jnp.float32)[0:8]

    rolled = [pltpu.roll(units[d], LANES - g * groups, 1) for d in range(chips)]
    for k in range(groups):
        at = slice(k * GROUP_ROWS, (k + 1) * GROUP_ROWS)
        total = [jnp.zeros((8, LANES), jnp.float32)] * ROWS
        for d in range(chips):
            unit = jnp.broadcast_to(rolled[d][:, k : k + 1], (8, LANES))
            code = r_ref[d, at, :].astype(jnp.float32)
            for s in range(ROWS):
                part = code[8 * s : 8 * s + 8]
                size = jnp.floor(jnp.log2(jnp.abs(part)) * STEPS + (OFFSET * STEPS + 0.5))
                total[s] = total[s] + size * jnp.where(part < 0, -unit, unit)
        o_ref[0, at, :] = jnp.concatenate(requantized(total), axis=0).astype(jnp.bfloat16)


def first_kernel(nodes, groups, after_ref, x_ref, o_ref, scratch):
    del after_ref

    def step(n, carry):
        for k in range(groups):
            at = pl.multiple_of((n * groups + k) * GROUP, GROUP)
            scratch[k] = x_ref[0:1, pl.ds(at, GROUP)].astype(jnp.float32).reshape(GROUP_ROWS, LANES)
        for k in range(groups):
            parts = [scratch[k, pl.ds(s, 8, stride=ROWS), :] for s in range(ROWS)]
            done = jnp.concatenate(requantized(parts), axis=0)
            o_ref[n, 0, k * GROUP_ROWS : (k + 1) * GROUP_ROWS, :] = done.astype(jnp.bfloat16)
        return carry

    lax.fori_loop(0, nodes, step, 0)


def second_kernel(nodes, groups, r_ref, o_ref):
    for k in range(groups):
        rows = slice(k * GROUP_ROWS, (k + 1) * GROUP_ROWS)
        total = r_ref[0, 0, rows, :].astype(jnp.float32)
        for n in range(1, nodes):
            total = total + r_ref[n, 0, rows, :].astype(jnp.float32)
        parts = [total[8 * s : 8 * s + 8] for s in range(ROWS)]
        o_ref[0, rows, :] = jnp.concatenate(requantized(parts), axis=0).astype(jnp.bfloat16)


def update_kernel(replicas, groups, r_ref, p_ref, m_ref, v_ref, po_ref, mo_ref, vo_ref, scratch):
    for k in range(groups):
        rows = slice(k * GROUP_ROWS, (k + 1) * GROUP_ROWS)
        total = r_ref[0, rows, :].astype(jnp.float32)
        for g in range(1, replicas):
            total = total + r_ref[g, rows, :].astype(jnp.float32)
        for s in range(ROWS):
            scratch[pl.ds(k * GROUP_ROWS + s, 8, stride=ROWS), :] = total[8 * s : 8 * s + 8]
    gradient = scratch[...]
    master = p_ref[...]
    moment = 0.9 * m_ref[...] + 0.1 * gradient
    second = 0.95 * v_ref[...] + 0.05 * gradient * gradient
    mo_ref[...] = moment
    vo_ref[...] = second
    po_ref[...] = master - 0.02 * (moment / (jnp.sqrt(second) + 1e-08) + 0.1 * master)


COST = pl.CostEstimate(flops=1, bytes_accessed=1, transcendentals=0)


def pair_sums(grads, start, count, replicas, chips, shard, before):
    rows, groups = shard // LANES, shard // GROUP
    nodes = 2 * chips
    core = lax.axis_index("core").astype(jnp.int32).reshape(1)
    half = jax.ShapeDtypeStruct((chips, count, rows, LANES), jnp.bfloat16)
    half_spec = pl.BlockSpec((chips, 1, rows, LANES), lambda g: (0, g, 0, 0))
    tile_spec = pl.BlockSpec((1, 8, LANES), lambda g: (g, 0, 0))
    own, send, scales = pl.pallas_call(
        lambda *refs: pair_kernel(chips, groups, *refs),
        name="quantize",
        grid=(count,),
        in_specs=[
            pl.BlockSpec(memory_space=pltpu.SMEM),
            pl.BlockSpec((1, nodes * shard), lambda g: (0, g + start)),
            pl.BlockSpec(memory_space=pl.ANY),
        ],
        out_specs=[half_spec, half_spec, tile_spec],
        out_shape=[half, half, jax.ShapeDtypeStruct((count, 8, LANES), jnp.float32)],
        scratch_shapes=[pltpu.VMEM((chips, 2 * groups, GROUP_ROWS, LANES), jnp.float32)],
        compiler_params=PARAMS,
        cost_estimate=COST,
    )(core, grads, before)
    swap = [(0, 1), (1, 0)]
    peer_scales = lax.ppermute(scales, "core", swap)
    peer = lax.ppermute(send, "core", swap)
    flag = jax.ShapeDtypeStruct((8, LANES), jnp.float32)
    whole = pl.BlockSpec((8, LANES), lambda g: (0, 0))
    return pl.pallas_call(
        lambda *refs: encode_kernel(chips, groups, count, *refs),
        name="add_and_encode",
        grid=(count,),
        in_specs=[half_spec, half_spec, tile_spec, tile_spec, whole],
        out_specs=[pl.BlockSpec(memory_space=pl.ANY), whole],
        out_shape=[
            jax.ShapeDtypeStruct((chips, count * rows + AUX_ROWS, LANES), jnp.bfloat16), flag,
        ],
        scratch_shapes=[
            pltpu.VMEM((2, chips, rows, LANES), jnp.bfloat16),
            pltpu.VMEM((chips, AUX_ROWS, LANES), jnp.bfloat16),
            pltpu.VMEM((chips, 8, LANES), jnp.float32),
            pltpu.VMEM((8, LANES), jnp.float32),
            pltpu.SemaphoreType.DMA((2,)),
            pltpu.SemaphoreType.DMA,
        ],
        compiler_params=PARAMS,
        cost_estimate=COST,
    )(own, peer, scales, peer_scales, before)


def node_sums(received, count, chips, shard):
    rows, groups = shard // LANES, shard // GROUP
    return pl.pallas_call(
        lambda *refs: decode_kernel(chips, groups, *refs),
        name="decode_and_requantize",
        grid=(count,),
        in_specs=[
            pl.BlockSpec((chips, rows, LANES), lambda g: (0, g, 0)),
            pl.BlockSpec((chips, AUX_ROWS, LANES), lambda g: (0, count * rows // AUX_ROWS, 0)),
        ],
        out_specs=pl.BlockSpec((1, rows, LANES), lambda g: (g, 0, 0)),
        out_shape=jax.ShapeDtypeStruct((count, rows, LANES), jnp.bfloat16),
        scratch_shapes=[pltpu.VMEM((chips, 8, LANES), jnp.float32)],
        compiler_params=PARAMS,
        cost_estimate=COST,
    )(received, received)


def plain_sums(grads, after, replicas, nodes, shard):
    rows, groups = shard // LANES, shard // GROUP
    first = pl.pallas_call(
        lambda *refs: first_kernel(nodes, groups, *refs),
        name="plain_quantize",
        grid=(replicas,),
        in_specs=[
            pl.BlockSpec(memory_space=pltpu.SMEM),
            pl.BlockSpec((1, nodes * shard), lambda g: (0, g)),
        ],
        out_specs=pl.BlockSpec((nodes, 1, rows, LANES), lambda g: (0, g, 0, 0)),
        out_shape=jax.ShapeDtypeStruct((nodes, replicas, rows, LANES), jnp.bfloat16),
        scratch_shapes=[pltpu.VMEM((groups, GROUP_ROWS, LANES), jnp.float32)],
        compiler_params=PARAMS,
    )(after, grads)
    received = lax.all_to_all(first, ("chip", "core"), split_axis=0, concat_axis=0, tiled=True)
    partial = pl.pallas_call(
        lambda *refs: second_kernel(nodes, groups, *refs),
        name="plain_requantize",
        grid=(replicas,),
        in_specs=[pl.BlockSpec((nodes, 1, rows, LANES), lambda g: (0, g, 0, 0))],
        out_specs=pl.BlockSpec((1, rows, LANES), lambda g: (g, 0, 0)),
        out_shape=jax.ShapeDtypeStruct((replicas, rows, LANES), jnp.bfloat16),
        compiler_params=PARAMS,
    )(received)
    return lax.all_to_all(partial, "group", split_axis=0, concat_axis=0, tiled=True)


def update(owned, master, moment, second):
    replicas, rows = owned.shape[:2]
    state = jax.ShapeDtypeStruct((rows, LANES), jnp.float32)
    return pl.pallas_call(
        lambda *refs: update_kernel(replicas, rows // GROUP_ROWS, *refs),
        name="adamw_update",
        out_shape=(state, state, state),
        scratch_shapes=[pltpu.VMEM((rows, LANES), jnp.float32)],
        compiler_params=PARAMS,
    )(owned, master, moment, second)


def body(grads, master, moment, second):
    replicas = lax.axis_size("group")
    chips = lax.axis_size("chip")
    shard = master.shape[0]
    flag = jnp.zeros((8, LANES), jnp.float32)
    partials, start = [], 0
    for count in PARTS:
        message, flag = pair_sums(grads, start, count, replicas, chips, shard, flag)
        received = lax.all_to_all(message, "chip", split_axis=0, concat_axis=0, tiled=True)
        partials.append(node_sums(received, count, chips, shard))
        start += count
    partial = jnp.concatenate(partials, axis=0) + partials[-1][0, 0, 0] * 0
    owned = lax.all_to_all(partial, "group", split_axis=0, concat_axis=0, tiled=True)
    state = [a.reshape(shard // LANES, LANES) for a in (master, moment, second)]
    owned, _ = lax.while_loop(
        lambda carry: jnp.logical_and(carry[1] == 0, jnp.any(jnp.isnan(carry[0][:, 0, 0]))),
        lambda carry: (
            plain_sums(grads, carry[1].reshape(1), replicas, 2 * chips, shard), carry[1] + 1,
        ),
        (owned, jnp.int32(0)),
    )
    return tuple(a.reshape(shard) for a in update(owned, *state))


def solution(mesh):
    groups, nodes = mesh.devices.shape
    cores = Mesh(mesh.devices.reshape(groups, nodes // 2, 2), ("group", "chip", "core"))
    split = P(("group", "chip", "core"))
    in_specs = (P(("group", "chip", "core"), None), split, split, split)
    return jax.shard_map(
        body, mesh=cores, in_specs=in_specs, out_specs=(split, split, split), check_vma=False
    )
```

```python
import jax
import jax.numpy as jnp
from jax import lax
from jax.experimental import pallas as pl
from jax.experimental.pallas import tpu as pltpu
from jax.sharding import Mesh
from jax.sharding import PartitionSpec as P

BLOCK = 512
LANES = 128
ROWS = BLOCK // LANES
GROUP_ROWS = 8 * ROWS
GROUP = GROUP_ROWS * LANES
SEND_LANE = 64
AUX_ROWS = 16

RATIO = 64.0
STEPS = 72.0
OFFSET = 113.0

PARTS = (3, 5, 8)
PIECES = 4
PARAMS = pltpu.CompilerParams(vmem_limit_bytes=48 << 20)
PARAMS_Q = pltpu.CompilerParams(vmem_limit_bytes=48 << 20)
PARAMS_C = pltpu.CompilerParams(vmem_limit_bytes=48 << 20)


def scale_of(peak):
    scale = jnp.full(peak.shape, 2.0**-24, jnp.float32)
    inverse = jnp.full(peak.shape, 2.0**24, jnp.float32)
    for k in (16, 8, 4, 2, 1):
        above = peak > scale * (127.0 * 2.0 ** (k - 1))
        scale = jnp.where(above, scale * 2.0**k, scale)
        inverse = jnp.where(above, inverse * 2.0**-k, inverse)
    return scale, inverse


def peak_of(parts):
    peak = jnp.abs(parts[0])
    for part in parts[1:]:
        peak = jnp.maximum(peak, jnp.abs(part))
    return jnp.max(peak, axis=1, keepdims=True)


def requantized(parts):
    scale, inverse = scale_of(jnp.broadcast_to(peak_of(parts), parts[0].shape))
    return [jnp.floor(part * inverse + 0.5) * scale for part in parts]


def pair_kernel(chips, groups, core_ref, x_ref, after_ref, own_ref, *refs):
    del after_ref
    *send_refs, scale_ref, scratch = refs
    core = core_ref[0]
    lane = lax.broadcasted_iota(jnp.int32, (8, LANES), 1)
    where = [(d, half, k) for d in range(chips) for half in range(2) for k in range(groups)]

    for d, half, k in where:
        node = 2 * d + (core if half == 0 else 1 - core)
        at = pl.multiple_of((node * groups + k) * GROUP, GROUP)
        rows = x_ref[0:1, pl.ds(at, GROUP)].astype(jnp.float32).reshape(GROUP_ROWS, LANES)
        scratch[d, half * groups + k] = rows

    def parts_of(d, half, k):
        return [scratch[d, half * groups + k, pl.ds(s, 8, stride=ROWS), :] for s in range(ROWS)]

    tiles = [jnp.zeros((8, LANES), jnp.float32)] * groups
    for d, half, k in where:
        column = lane == half * SEND_LANE + d * groups + k
        tiles[k] = jnp.where(column, peak_of(parts_of(d, half, k)), tiles[k])
    tile = tiles[0]
    for k in range(1, groups):
        tile = jnp.maximum(tile, tiles[k])
    scale, inverse = scale_of(tile)
    scale_ref[0] = jnp.where(tile > 0, scale, 0.0)

    for d, half, k in where:
        at = half * SEND_LANE + d * groups + k
        s_col = jnp.broadcast_to(scale[:, at : at + 1], (8, LANES))
        i_col = jnp.broadcast_to(inverse[:, at : at + 1], (8, LANES))
        done = [jnp.floor(part * i_col + 0.5) * s_col for part in parts_of(d, half, k)]
        o_ref, slot = (send_refs[d % PIECES], d // PIECES) if half else (own_ref, d)
        at = slice(k * GROUP_ROWS, (k + 1) * GROUP_ROWS)
        o_ref[slot, 0, at, :] = jnp.concatenate(done, axis=0).astype(jnp.bfloat16)


def encode_kernel(
    chips, groups, count, own_ref, mine_ref, theirs_ref, before_ref, *refs
):
    *peer_refs, m_ref, flag_ref, buffer, aux, packed, bad, sems, aux_sem = refs
    g = pl.program_id(0)
    slot = lax.rem(g, 2)
    rows = groups * GROUP_ROWS
    lane = lax.broadcasted_iota(jnp.int32, (8, LANES), 1)

    def copy(step, at):
        where = m_ref.at[:, pl.ds(pl.multiple_of(step * rows, rows), rows), :]
        return pltpu.make_async_copy(buffer.at[at], where, sems.at[at])

    @pl.when(g == 0)
    def _():
        bad[...] = before_ref[...]
        packed[...] = jnp.ones_like(packed)

    @pl.when(g >= 2)
    def _():
        copy(g - 2, slot).wait()

    mine, theirs = mine_ref[0], pltpu.roll(theirs_ref[0], SEND_LANE, 1)
    high, low = jnp.maximum(mine, theirs), jnp.minimum(mine, theirs)
    bad[...] = jnp.where((low > 0) & (high > RATIO * low), 1.0, bad[...])
    scale, inverse = scale_of(127.0 * high)
    weight = inverse * (RATIO / STEPS)

    for d in range(chips):
        tile = packed[d]
        for k in range(groups):
            column = slice(d * groups + k, d * groups + k + 1)
            tile = jnp.where(lane == g * groups + k, scale[:, column], tile)
            w_col = jnp.broadcast_to(weight[:, column], (8, LANES))
            at = slice(k * GROUP_ROWS, (k + 1) * GROUP_ROWS)
            peer = peer_refs[d % PIECES][d // PIECES, 0, at, :].astype(jnp.float32)
            total = own_ref[d, 0, at, :].astype(jnp.float32) + peer
            out = []
            for s in range(ROWS):
                part = total[8 * s : 8 * s + 8]
                code = jnp.exp2(jnp.abs(part) * w_col - OFFSET)
                out.append(jnp.where(part < 0, -code, code))
            buffer[slot, d, at, :] = jnp.concatenate(out, axis=0).astype(jnp.bfloat16)
        packed[d] = tile
    copy(g, slot).start()

    @pl.when(g == count - 1)
    def _():
        flag = jnp.max(bad[...])
        flag_ref[...] = bad[...]
        for d in range(chips):
            unit = packed[d] * jnp.where(flag > 0, jnp.float32(jnp.nan), 1.0 / RATIO)
            aux[d] = jnp.concatenate([unit, unit], axis=0).astype(jnp.bfloat16)
        last = pltpu.make_async_copy(aux, m_ref.at[:, pl.ds(count * rows, AUX_ROWS), :], aux_sem)
        last.start()
        last.wait()
        if count >= 2:
            copy(g - 1, 1 - slot).wait()
        copy(g, slot).wait()


def decode_kernel(chips, groups, r_ref, aux_ref, o_ref, units):
    g = pl.program_id(0)

    @pl.when(g == 0)
    def _():
        for d in range(chips):
            units[d] = aux_ref[d].astype(jnp.float32)[0:8]

    rolled = [pltpu.roll(units[d], LANES - g * groups, 1) for d in range(chips)]
    for k in range(groups):
        at = slice(k * GROUP_ROWS, (k + 1) * GROUP_ROWS)
        total = [jnp.zeros((8, LANES), jnp.float32)] * ROWS
        for d in range(chips):
            unit = jnp.broadcast_to(rolled[d][:, k : k + 1], (8, LANES))
            code = r_ref[d, at, :].astype(jnp.float32)
            for s in range(ROWS):
                part = code[8 * s : 8 * s + 8]
                size = jnp.floor(jnp.log2(jnp.abs(part)) * STEPS + (OFFSET * STEPS + 0.5))
                total[s] = total[s] + size * jnp.where(part < 0, -unit, unit)
        o_ref[0, at, :] = jnp.concatenate(requantized(total), axis=0).astype(jnp.bfloat16)


def first_kernel(nodes, groups, after_ref, x_ref, o_ref, scratch):
    del after_ref

    def step(n, carry):
        for k in range(groups):
            at = pl.multiple_of((n * groups + k) * GROUP, GROUP)
            scratch[k] = x_ref[0:1, pl.ds(at, GROUP)].astype(jnp.float32).reshape(GROUP_ROWS, LANES)
        for k in range(groups):
            parts = [scratch[k, pl.ds(s, 8, stride=ROWS), :] for s in range(ROWS)]
            done = jnp.concatenate(requantized(parts), axis=0)
            o_ref[n, 0, k * GROUP_ROWS : (k + 1) * GROUP_ROWS, :] = done.astype(jnp.bfloat16)
        return carry

    lax.fori_loop(0, nodes, step, 0)


def second_kernel(nodes, groups, r_ref, o_ref):
    for k in range(groups):
        rows = slice(k * GROUP_ROWS, (k + 1) * GROUP_ROWS)
        total = r_ref[0, 0, rows, :].astype(jnp.float32)
        for n in range(1, nodes):
            total = total + r_ref[n, 0, rows, :].astype(jnp.float32)
        parts = [total[8 * s : 8 * s + 8] for s in range(ROWS)]
        o_ref[0, rows, :] = jnp.concatenate(requantized(parts), axis=0).astype(jnp.bfloat16)


def update_kernel(replicas, groups, r_ref, p_ref, m_ref, v_ref, po_ref, mo_ref, vo_ref, scratch):
    for k in range(groups):
        rows = slice(k * GROUP_ROWS, (k + 1) * GROUP_ROWS)
        total = r_ref[0, rows, :].astype(jnp.float32)
        for g in range(1, replicas):
            total = total + r_ref[g, rows, :].astype(jnp.float32)
        for s in range(ROWS):
            scratch[pl.ds(k * GROUP_ROWS + s, 8, stride=ROWS), :] = total[8 * s : 8 * s + 8]
    gradient = scratch[...]
    master = p_ref[...]
    moment = 0.9 * m_ref[...] + 0.1 * gradient
    second = 0.95 * v_ref[...] + 0.05 * gradient * gradient
    mo_ref[...] = moment
    vo_ref[...] = second
    po_ref[...] = master - 0.02 * (moment / (jnp.sqrt(second) + 1e-08) + 0.1 * master)


COST = pl.CostEstimate(flops=1, bytes_accessed=1, transcendentals=0)


def quantized(grads, after, start, count, chips, shard):
    rows, groups = shard // LANES, shard // GROUP
    core = lax.axis_index("core").astype(jnp.int32).reshape(1)

    def block(size):
        shape = jax.ShapeDtypeStruct((size, count, rows, LANES), jnp.bfloat16)
        return shape, pl.BlockSpec((size, 1, rows, LANES), lambda g: (0, g, 0, 0))

    blocks = [block(chips)] + [block(chips // PIECES)] * PIECES
    tiles = jax.ShapeDtypeStruct((count, 8, LANES), jnp.float32)
    own, *send, scales = pl.pallas_call(
        lambda *refs: pair_kernel(chips, groups, *refs),
        name="quantize",
        grid=(count,),
        in_specs=[
            pl.BlockSpec(memory_space=pltpu.SMEM),
            pl.BlockSpec((1, 2 * chips * shard), lambda g: (0, g + start)),
            pl.BlockSpec(memory_space=pl.ANY),
        ],
        out_specs=[b for _, b in blocks] + [pl.BlockSpec((1, 8, LANES), lambda g: (g, 0, 0))],
        out_shape=[a for a, _ in blocks] + [tiles],
        scratch_shapes=[pltpu.VMEM((chips, 2 * groups, GROUP_ROWS, LANES), jnp.float32)],
        compiler_params=PARAMS_Q,
        cost_estimate=COST,
    )(core, grads, after)
    peer, peer_scales = jax.tree.map(lambda a: lax.ppermute(a, "core", [(0, 1), (1, 0)]), (send, scales))
    return own, peer, scales, peer_scales


def pair_sums(own, peer, scales, peer_scales, before, after=()):
    chips, count, rows = own.shape[:3]
    half_spec = pl.BlockSpec((chips, 1, rows, LANES), lambda g: (0, g, 0, 0))
    piece_spec = pl.BlockSpec((chips // PIECES, 1, rows, LANES), lambda g: (0, g, 0, 0))
    tile_spec = pl.BlockSpec((1, 8, LANES), lambda g: (g, 0, 0))
    flag = jax.ShapeDtypeStruct((8, LANES), jnp.float32)
    whole = pl.BlockSpec((8, LANES), lambda g: (0, 0))
    return pl.pallas_call(
        lambda *refs: encode_kernel(chips, rows // GROUP_ROWS, count, *refs),
        name="add_and_encode",
        grid=(count,),
        in_specs=[half_spec, tile_spec, tile_spec, whole] + [piece_spec] * PIECES,
        out_specs=[pl.BlockSpec(memory_space=pl.ANY), whole],
        out_shape=[
            jax.ShapeDtypeStruct((chips, count * rows + AUX_ROWS, LANES), jnp.bfloat16), flag,
        ],
        scratch_shapes=[
            pltpu.VMEM((2, chips, rows, LANES), jnp.bfloat16),
            pltpu.VMEM((chips, AUX_ROWS, LANES), jnp.bfloat16),
            pltpu.VMEM((chips, 8, LANES), jnp.float32),
            pltpu.VMEM((8, LANES), jnp.float32),
            pltpu.SemaphoreType.DMA((2,)),
            pltpu.SemaphoreType.DMA,
        ],
        compiler_params=PARAMS_C,
        cost_estimate=COST,
    )(own, scales, peer_scales, before, *peer)


def node_sums(received, count, chips, shard):
    rows, groups = shard // LANES, shard // GROUP
    return pl.pallas_call(
        lambda *refs: decode_kernel(chips, groups, *refs),
        name="decode_and_requantize",
        grid=(count,),
        in_specs=[
            pl.BlockSpec((chips, rows, LANES), lambda g: (0, g, 0)),
            pl.BlockSpec((chips, AUX_ROWS, LANES), lambda g: (0, count * rows // AUX_ROWS, 0)),
        ],
        out_specs=pl.BlockSpec((1, rows, LANES), lambda g: (g, 0, 0)),
        out_shape=jax.ShapeDtypeStruct((count, rows, LANES), jnp.bfloat16),
        scratch_shapes=[pltpu.VMEM((chips, 8, LANES), jnp.float32)],
        compiler_params=PARAMS,
        cost_estimate=COST,
    )(received, received)


def plain_sums(grads, after, replicas, nodes, shard):
    rows, groups = shard // LANES, shard // GROUP
    first = pl.pallas_call(
        lambda *refs: first_kernel(nodes, groups, *refs),
        name="plain_quantize",
        grid=(replicas,),
        in_specs=[
            pl.BlockSpec(memory_space=pltpu.SMEM),
            pl.BlockSpec((1, nodes * shard), lambda g: (0, g)),
        ],
        out_specs=pl.BlockSpec((nodes, 1, rows, LANES), lambda g: (0, g, 0, 0)),
        out_shape=jax.ShapeDtypeStruct((nodes, replicas, rows, LANES), jnp.bfloat16),
        scratch_shapes=[pltpu.VMEM((groups, GROUP_ROWS, LANES), jnp.float32)],
        compiler_params=PARAMS,
    )(after, grads)
    received = lax.all_to_all(first, ("chip", "core"), split_axis=0, concat_axis=0, tiled=True)
    partial = pl.pallas_call(
        lambda *refs: second_kernel(nodes, groups, *refs),
        name="plain_requantize",
        grid=(replicas,),
        in_specs=[pl.BlockSpec((nodes, 1, rows, LANES), lambda g: (0, g, 0, 0))],
        out_specs=pl.BlockSpec((1, rows, LANES), lambda g: (g, 0, 0)),
        out_shape=jax.ShapeDtypeStruct((replicas, rows, LANES), jnp.bfloat16),
        compiler_params=PARAMS,
    )(received)
    return lax.all_to_all(partial, "group", split_axis=0, concat_axis=0, tiled=True)


def update(owned, master, moment, second):
    replicas, rows = owned.shape[:2]
    state = jax.ShapeDtypeStruct((rows, LANES), jnp.float32)
    return pl.pallas_call(
        lambda *refs: update_kernel(replicas, rows // GROUP_ROWS, *refs),
        name="adamw_update",
        out_shape=(state, state, state),
        scratch_shapes=[pltpu.VMEM((rows, LANES), jnp.float32)],
        compiler_params=PARAMS,
    )(owned, master, moment, second)


def body(grads, master, moment, second):
    replicas = lax.axis_size("group")
    chips = lax.axis_size("chip")
    shard = master.shape[0]
    flag = jnp.zeros((8, LANES), jnp.float32)
    partials, start = [], 0
    for count in PARTS:
        message, flag = pair_sums(*quantized(grads, flag, start, count, chips, shard), flag)
        received = lax.all_to_all(message, "chip", split_axis=0, concat_axis=0, tiled=True)
        partials.append(node_sums(received, count, chips, shard))
        start += count
    partial = jnp.concatenate(partials, axis=0) + partials[-1][0, 0, 0] * 0
    owned = lax.all_to_all(partial, "group", split_axis=0, concat_axis=0, tiled=True)
    state = [a.reshape(shard // LANES, LANES) for a in (master, moment, second)]
    owned, _ = lax.while_loop(
        lambda carry: jnp.logical_and(carry[1] == 0, jnp.any(jnp.isnan(carry[0][:, 0, 0]))),
        lambda carry: (
            plain_sums(grads, carry[1].reshape(1), replicas, 2 * chips, shard), carry[1] + 1,
        ),
        (owned, jnp.int32(0)),
    )
    return tuple(a.reshape(shard) for a in update(owned, *state))


def solution(mesh):
    groups, nodes = mesh.devices.shape
    cores = Mesh(mesh.devices.reshape(groups, nodes // 2, 2), ("group", "chip", "core"))
    split = P(("group", "chip", "core"))
    in_specs = (P(("group", "chip", "core"), None), split, split, split)
    return jax.shard_map(
        body, mesh=cores, in_specs=in_specs, out_specs=(split, split, split), check_vma=False
    )
```

```python
import jax
import jax.numpy as jnp
from jax import lax
from jax.experimental import pallas as pl
from jax.experimental.pallas import tpu as pltpu
from jax.sharding import Mesh
from jax.sharding import PartitionSpec as P

BLOCK = 512
LANES = 128
ROWS = BLOCK // LANES
GROUP_ROWS = 8 * ROWS
GROUP = GROUP_ROWS * LANES
SEND_LANE = 64
AUX_ROWS = 16

RATIO = 64.0
STEPS = 72.0
OFFSET = 113.0

PARTS = (5, 6, 5)
PIECES = 2
PARAMS = pltpu.CompilerParams(vmem_limit_bytes=48 << 20)
PARAMS_Q = pltpu.CompilerParams(vmem_limit_bytes=48 << 20)
PARAMS_C = pltpu.CompilerParams(vmem_limit_bytes=48 << 20)


def scale_of(peak):
    scale = jnp.full(peak.shape, 2.0**-24, jnp.float32)
    inverse = jnp.full(peak.shape, 2.0**24, jnp.float32)
    for k in (16, 8, 4, 2, 1):
        above = peak > scale * (127.0 * 2.0 ** (k - 1))
        scale = jnp.where(above, scale * 2.0**k, scale)
        inverse = jnp.where(above, inverse * 2.0**-k, inverse)
    return scale, inverse


def peak_of(parts):
    peak = jnp.abs(parts[0])
    for part in parts[1:]:
        peak = jnp.maximum(peak, jnp.abs(part))
    return jnp.max(peak, axis=1, keepdims=True)


def requantized(parts):
    scale, inverse = scale_of(jnp.broadcast_to(peak_of(parts), parts[0].shape))
    return [jnp.floor(part * inverse + 0.5) * scale for part in parts]


def pair_kernel(chips, groups, core_ref, x_ref, after_ref, own_ref, *refs):
    del after_ref
    *send_refs, scale_ref, scratch = refs
    core = core_ref[0]
    lane = lax.broadcasted_iota(jnp.int32, (8, LANES), 1)
    where = [(d, half, k) for d in range(chips) for half in range(2) for k in range(groups)]

    for d, half, k in where:
        node = 2 * d + (core if half == 0 else 1 - core)
        at = pl.multiple_of((node * groups + k) * GROUP, GROUP)
        rows = x_ref[0:1, pl.ds(at, GROUP)].astype(jnp.float32).reshape(GROUP_ROWS, LANES)
        scratch[d, half * groups + k] = rows

    def parts_of(d, half, k):
        return [scratch[d, half * groups + k, pl.ds(s, 8, stride=ROWS), :] for s in range(ROWS)]

    tiles = [jnp.zeros((8, LANES), jnp.float32)] * groups
    for d, half, k in where:
        column = lane == half * SEND_LANE + d * groups + k
        tiles[k] = jnp.where(column, peak_of(parts_of(d, half, k)), tiles[k])
    tile = tiles[0]
    for k in range(1, groups):
        tile = jnp.maximum(tile, tiles[k])
    scale, inverse = scale_of(tile)
    scale_ref[0] = jnp.where(tile > 0, scale, 0.0)

    for d, half, k in where:
        at = half * SEND_LANE + d * groups + k
        s_col = jnp.broadcast_to(scale[:, at : at + 1], (8, LANES))
        i_col = jnp.broadcast_to(inverse[:, at : at + 1], (8, LANES))
        done = [jnp.floor(part * i_col + 0.5) * s_col for part in parts_of(d, half, k)]
        o_ref, slot = (send_refs[d % PIECES], d // PIECES) if half else (own_ref, d)
        at = slice(k * GROUP_ROWS, (k + 1) * GROUP_ROWS)
        o_ref[slot, 0, at, :] = jnp.concatenate(done, axis=0).astype(jnp.bfloat16)


def encode_kernel(
    chips, groups, count, own_ref, mine_ref, theirs_ref, before_ref, *refs
):
    *peer_refs, m_ref, flag_ref, buffer, aux, packed, bad, sems, aux_sem = refs
    g = pl.program_id(0)
    slot = lax.rem(g, 2)
    rows = groups * GROUP_ROWS
    lane = lax.broadcasted_iota(jnp.int32, (8, LANES), 1)

    def copy(step, at):
        where = m_ref.at[:, pl.ds(pl.multiple_of(step * rows, rows), rows), :]
        return pltpu.make_async_copy(buffer.at[at], where, sems.at[at])

    @pl.when(g == 0)
    def _():
        bad[...] = before_ref[...]
        packed[...] = jnp.ones_like(packed)

    @pl.when(g >= 2)
    def _():
        copy(g - 2, slot).wait()

    mine, theirs = mine_ref[0], pltpu.roll(theirs_ref[0], SEND_LANE, 1)
    high, low = jnp.maximum(mine, theirs), jnp.minimum(mine, theirs)
    bad[...] = jnp.where((low > 0) & (high > RATIO * low), 1.0, bad[...])
    scale, inverse = scale_of(127.0 * high)
    weight = inverse * (RATIO / STEPS)

    for d in range(chips):
        tile = packed[d]
        for k in range(groups):
            column = slice(d * groups + k, d * groups + k + 1)
            tile = jnp.where(lane == g * groups + k, scale[:, column], tile)
            w_col = jnp.broadcast_to(weight[:, column], (8, LANES))
            at = slice(k * GROUP_ROWS, (k + 1) * GROUP_ROWS)
            peer = peer_refs[d % PIECES][d // PIECES, 0, at, :].astype(jnp.float32)
            total = own_ref[d, 0, at, :].astype(jnp.float32) + peer
            out = []
            for s in range(ROWS):
                part = total[8 * s : 8 * s + 8]
                code = jnp.exp2(jnp.abs(part) * w_col - OFFSET)
                out.append(jnp.where(part < 0, -code, code))
            buffer[slot, d, at, :] = jnp.concatenate(out, axis=0).astype(jnp.bfloat16)
        packed[d] = tile
    copy(g, slot).start()

    @pl.when(g == count - 1)
    def _():
        flag = jnp.max(bad[...])
        flag_ref[...] = bad[...]
        for d in range(chips):
            unit = packed[d] * jnp.where(flag > 0, jnp.float32(jnp.nan), 1.0 / RATIO)
            aux[d] = jnp.concatenate([unit, unit], axis=0).astype(jnp.bfloat16)
        last = pltpu.make_async_copy(aux, m_ref.at[:, pl.ds(count * rows, AUX_ROWS), :], aux_sem)
        last.start()
        last.wait()
        if count >= 2:
            copy(g - 1, 1 - slot).wait()
        copy(g, slot).wait()


def decode_kernel(chips, groups, start, final, r_ref, aux_ref, before_ref, o_ref, buffer, units, sems, bad):
    del before_ref
    g, count = pl.program_id(0), pl.num_programs(0)
    slot = lax.rem(g, 2)

    def copy(step, at):
        return pltpu.make_async_copy(buffer.at[at], o_ref.at[step + start], sems.at[at])

    @pl.when(g == 0)
    def _():
        for d in range(chips):
            units[d] = aux_ref[d].astype(jnp.float32)[0:8]

    @pl.when(g >= 2)
    def _():
        copy(g - 2, slot).wait()

    rolled = [pltpu.roll(units[d], LANES - g * groups, 1) for d in range(chips)]
    for k in range(groups):
        at = slice(k * GROUP_ROWS, (k + 1) * GROUP_ROWS)
        total = [jnp.zeros((8, LANES), jnp.float32)] * ROWS
        for d in range(chips):
            unit = jnp.broadcast_to(rolled[d][:, k : k + 1], (8, LANES))
            code = r_ref[d, at, :].astype(jnp.float32)
            for s in range(ROWS):
                part = code[8 * s : 8 * s + 8]
                size = jnp.floor(jnp.log2(jnp.abs(part)) * STEPS + (OFFSET * STEPS + 0.5))
                total[s] = total[s] + size * jnp.where(part < 0, -unit, unit)
        buffer[slot, at, :] = jnp.concatenate(requantized(total), axis=0).astype(jnp.bfloat16)
    copy(g, slot).start()

    @pl.when(g == count - 1)
    def _():
        @pl.when(count >= 2)
        def _():
            copy(g - 1, 1 - slot).wait()

        copy(g, slot).wait()
        if final:
            total = units[0]
            for d in range(1, chips):
                total = total + units[d]

            @pl.when(jnp.max(jnp.where(jnp.isnan(total), 1.0, 0.0)) > 0)
            def _():
                buffer[0] = jnp.full(buffer.shape[1:], jnp.nan, jnp.bfloat16)

                def spoil(j, carry):
                    one = pltpu.make_async_copy(buffer.at[0], o_ref.at[j], bad)
                    one.start()
                    one.wait()
                    return carry

                lax.fori_loop(0, o_ref.shape[0], spoil, 0)


def first_kernel(nodes, groups, after_ref, x_ref, o_ref, scratch):
    del after_ref

    def step(n, carry):
        for k in range(groups):
            at = pl.multiple_of((n * groups + k) * GROUP, GROUP)
            scratch[k] = x_ref[0:1, pl.ds(at, GROUP)].astype(jnp.float32).reshape(GROUP_ROWS, LANES)
        for k in range(groups):
            parts = [scratch[k, pl.ds(s, 8, stride=ROWS), :] for s in range(ROWS)]
            done = jnp.concatenate(requantized(parts), axis=0)
            o_ref[n, 0, k * GROUP_ROWS : (k + 1) * GROUP_ROWS, :] = done.astype(jnp.bfloat16)
        return carry

    lax.fori_loop(0, nodes, step, 0)


def second_kernel(nodes, groups, r_ref, o_ref):
    for k in range(groups):
        rows = slice(k * GROUP_ROWS, (k + 1) * GROUP_ROWS)
        total = r_ref[0, 0, rows, :].astype(jnp.float32)
        for n in range(1, nodes):
            total = total + r_ref[n, 0, rows, :].astype(jnp.float32)
        parts = [total[8 * s : 8 * s + 8] for s in range(ROWS)]
        o_ref[0, rows, :] = jnp.concatenate(requantized(parts), axis=0).astype(jnp.bfloat16)


def update_kernel(replicas, groups, r_ref, p_ref, m_ref, v_ref, po_ref, mo_ref, vo_ref, bad_ref, scratch):
    for k in range(groups):
        rows = slice(k * GROUP_ROWS, (k + 1) * GROUP_ROWS)
        total = r_ref[0, rows, :].astype(jnp.float32)
        for g in range(1, replicas):
            total = total + r_ref[g, rows, :].astype(jnp.float32)
        for s in range(ROWS):
            scratch[pl.ds(k * GROUP_ROWS + s, 8, stride=ROWS), :] = total[8 * s : 8 * s + 8]
    gradient = scratch[...]
    master = p_ref[...]
    moment = 0.9 * m_ref[...] + 0.1 * gradient
    second = 0.95 * v_ref[...] + 0.05 * gradient * gradient
    mo_ref[...] = moment
    vo_ref[...] = second
    po_ref[...] = master - 0.02 * (moment / (jnp.sqrt(second) + 1e-08) + 0.1 * master)
    spoilt = jnp.max(jnp.where(jnp.isnan(gradient[0:8]), 1.0, 0.0))
    bad_ref[0] = jnp.where(spoilt > 0, 1, 0).astype(jnp.int32)


COST = pl.CostEstimate(flops=1, bytes_accessed=1, transcendentals=0)


def quantized(grads, after, start, count, chips, shard):
    rows, groups = shard // LANES, shard // GROUP
    core = lax.axis_index("core").astype(jnp.int32).reshape(1)

    def block(size):
        shape = jax.ShapeDtypeStruct((size, count, rows, LANES), jnp.bfloat16)
        return shape, pl.BlockSpec((size, 1, rows, LANES), lambda g: (0, g, 0, 0))

    blocks = [block(chips)] + [block(chips // PIECES)] * PIECES
    tiles = jax.ShapeDtypeStruct((count, 8, LANES), jnp.float32)
    own, *send, scales = pl.pallas_call(
        lambda *refs: pair_kernel(chips, groups, *refs),
        name="quantize",
        grid=(count,),
        in_specs=[
            pl.BlockSpec(memory_space=pltpu.SMEM),
            pl.BlockSpec((1, 2 * chips * shard), lambda g: (0, g + start)),
            pl.BlockSpec(memory_space=pl.ANY),
        ],
        out_specs=[b for _, b in blocks] + [pl.BlockSpec((1, 8, LANES), lambda g: (g, 0, 0))],
        out_shape=[a for a, _ in blocks] + [tiles],
        scratch_shapes=[pltpu.VMEM((chips, 2 * groups, GROUP_ROWS, LANES), jnp.float32)],
        compiler_params=PARAMS_Q,
        cost_estimate=COST,
    )(core, grads, after)
    peer, peer_scales = jax.tree.map(lambda a: lax.ppermute(a, "core", [(0, 1), (1, 0)]), (send, scales))
    return own, peer, scales, peer_scales


def pair_sums(own, peer, scales, peer_scales, before, after=()):
    chips, count, rows = own.shape[:3]
    half_spec = pl.BlockSpec((chips, 1, rows, LANES), lambda g: (0, g, 0, 0))
    piece_spec = pl.BlockSpec((chips // PIECES, 1, rows, LANES), lambda g: (0, g, 0, 0))
    tile_spec = pl.BlockSpec((1, 8, LANES), lambda g: (g, 0, 0))
    flag = jax.ShapeDtypeStruct((8, LANES), jnp.float32)
    whole = pl.BlockSpec((8, LANES), lambda g: (0, 0))
    return pl.pallas_call(
        lambda *refs: encode_kernel(chips, rows // GROUP_ROWS, count, *refs),
        name="add_and_encode",
        grid=(count,),
        in_specs=[half_spec, tile_spec, tile_spec, whole] + [piece_spec] * PIECES,
        out_specs=[pl.BlockSpec(memory_space=pl.ANY), whole],
        out_shape=[
            jax.ShapeDtypeStruct((chips, count * rows + AUX_ROWS, LANES), jnp.bfloat16), flag,
        ],
        scratch_shapes=[
            pltpu.VMEM((2, chips, rows, LANES), jnp.bfloat16),
            pltpu.VMEM((chips, AUX_ROWS, LANES), jnp.bfloat16),
            pltpu.VMEM((chips, 8, LANES), jnp.float32),
            pltpu.VMEM((8, LANES), jnp.float32),
            pltpu.SemaphoreType.DMA((2,)),
            pltpu.SemaphoreType.DMA,
        ],
        compiler_params=PARAMS_C,
        cost_estimate=COST,
    )(own, scales, peer_scales, before, *peer)


def node_sums(received, partial, start, count, chips, final):
    rows = partial.shape[1]
    return pl.pallas_call(
        lambda *refs: decode_kernel(chips, rows // GROUP_ROWS, start, final, *refs),
        name="decode_and_requantize",
        grid=(count,),
        in_specs=[
            pl.BlockSpec((chips, rows, LANES), lambda g: (0, g, 0)),
            pl.BlockSpec((chips, AUX_ROWS, LANES), lambda g: (0, count * rows // AUX_ROWS, 0)),
            pl.BlockSpec(memory_space=pl.ANY),
        ],
        out_specs=pl.BlockSpec(memory_space=pl.ANY),
        out_shape=jax.ShapeDtypeStruct(partial.shape, partial.dtype),
        scratch_shapes=[
            pltpu.VMEM((2, rows, LANES), jnp.bfloat16),
            pltpu.VMEM((chips, 8, LANES), jnp.float32),
            pltpu.SemaphoreType.DMA((2,)),
            pltpu.SemaphoreType.DMA,
        ],
        input_output_aliases={2: 0},
        compiler_params=PARAMS,
        cost_estimate=COST,
    )(received, received, partial)


def plain_sums(grads, after, replicas, nodes, shard):
    rows, groups = shard // LANES, shard // GROUP
    first = pl.pallas_call(
        lambda *refs: first_kernel(nodes, groups, *refs),
        name="plain_quantize",
        grid=(replicas,),
        in_specs=[
            pl.BlockSpec(memory_space=pltpu.SMEM),
            pl.BlockSpec((1, nodes * shard), lambda g: (0, g)),
        ],
        out_specs=pl.BlockSpec((nodes, 1, rows, LANES), lambda g: (0, g, 0, 0)),
        out_shape=jax.ShapeDtypeStruct((nodes, replicas, rows, LANES), jnp.bfloat16),
        scratch_shapes=[pltpu.VMEM((groups, GROUP_ROWS, LANES), jnp.float32)],
        compiler_params=PARAMS,
    )(after, grads)
    received = lax.all_to_all(first, ("chip", "core"), split_axis=0, concat_axis=0, tiled=True)
    partial = pl.pallas_call(
        lambda *refs: second_kernel(nodes, groups, *refs),
        name="plain_requantize",
        grid=(replicas,),
        in_specs=[pl.BlockSpec((nodes, 1, rows, LANES), lambda g: (0, g, 0, 0))],
        out_specs=pl.BlockSpec((1, rows, LANES), lambda g: (g, 0, 0)),
        out_shape=jax.ShapeDtypeStruct((replicas, rows, LANES), jnp.bfloat16),
        compiler_params=PARAMS,
    )(received)
    return lax.all_to_all(partial, "group", split_axis=0, concat_axis=0, tiled=True)


def update(owned, master, moment, second):
    replicas, rows = owned.shape[:2]
    state = jax.ShapeDtypeStruct((rows, LANES), jnp.float32)
    whole = pl.BlockSpec(memory_space=pltpu.VMEM)
    return pl.pallas_call(
        lambda *refs: update_kernel(replicas, rows // GROUP_ROWS, *refs),
        name="adamw_update",
        out_shape=(state, state, state, jax.ShapeDtypeStruct((1,), jnp.int32)),
        out_specs=(whole, whole, whole, pl.BlockSpec(memory_space=pltpu.SMEM)),
        scratch_shapes=[pltpu.VMEM((rows, LANES), jnp.float32)],
        compiler_params=PARAMS,
    )(owned, master, moment, second)


def body(grads, master, moment, second):
    replicas = lax.axis_size("group")
    chips = lax.axis_size("chip")
    shard = master.shape[0]
    flag = jnp.zeros((8, LANES), jnp.float32)
    partial = jnp.zeros((replicas, shard // LANES, LANES), jnp.bfloat16)
    start = 0
    for count in PARTS:
        message, flag = pair_sums(*quantized(grads, flag, start, count, chips, shard), flag)
        received = lax.all_to_all(message, "chip", split_axis=0, concat_axis=0, tiled=True)
        partial = node_sums(received, partial, start, count, chips, start + count == replicas)
        start += count
    owned = lax.all_to_all(partial, "group", split_axis=0, concat_axis=0, tiled=True)
    state = [a.reshape(shard // LANES, LANES) for a in (master, moment, second)]

    def general(carry):
        *_, done = update(plain_sums(grads, carry[3], replicas, 2 * chips, shard), *state)
        return (*_, jnp.zeros_like(done))

    *outs, _ = lax.while_loop(lambda carry: carry[3][0] > 0, general, update(owned, *state))
    return tuple(a.reshape(shard) for a in outs)


def solution(mesh):
    groups, nodes = mesh.devices.shape
    cores = Mesh(mesh.devices.reshape(groups, nodes // 2, 2), ("group", "chip", "core"))
    split = P(("group", "chip", "core"))
    in_specs = (P(("group", "chip", "core"), None), split, split, split)
    return jax.shard_map(
        body, mesh=cores, in_specs=in_specs, out_specs=(split, split, split), check_vma=False
    )
```

```python
import jax
import jax.numpy as jnp
from jax import lax
from jax.experimental import pallas as pl
from jax.experimental.pallas import tpu as pltpu
from jax.sharding import Mesh
from jax.sharding import PartitionSpec as P

BLOCK = 512
LANES = 128
ROWS = BLOCK // LANES
GROUP_ROWS = 8 * ROWS
GROUP = GROUP_ROWS * LANES
SEND_LANE = 64
AUX_ROWS = 16

RATIO = 64.0
STEPS = 72.0
OFFSET = 113.0

PARTS = (8, 8)
PIECES = 2
PARAMS = pltpu.CompilerParams(vmem_limit_bytes=48 << 20)
PARAMS_Q = pltpu.CompilerParams(vmem_limit_bytes=48 << 20)
PARAMS_C = pltpu.CompilerParams(vmem_limit_bytes=48 << 20)


def scale_of(peak):
    scale = jnp.full(peak.shape, 2.0**-24, jnp.float32)
    inverse = jnp.full(peak.shape, 2.0**24, jnp.float32)
    for k in (16, 8, 4, 2, 1):
        above = peak > scale * (127.0 * 2.0 ** (k - 1))
        scale = jnp.where(above, scale * 2.0**k, scale)
        inverse = jnp.where(above, inverse * 2.0**-k, inverse)
    return scale, inverse


def peak_of(parts):
    peak = jnp.abs(parts[0])
    for part in parts[1:]:
        peak = jnp.maximum(peak, jnp.abs(part))
    return jnp.max(peak, axis=1, keepdims=True)


def requantized(parts):
    scale, inverse = scale_of(jnp.broadcast_to(peak_of(parts), parts[0].shape))
    return [jnp.floor(part * inverse + 0.5) * scale for part in parts]


def pair_kernel(chips, groups, core_ref, x_ref, after_ref, own_ref, *refs):
    del after_ref
    *send_refs, scale_ref, scratch = refs
    core = core_ref[0]
    lane = lax.broadcasted_iota(jnp.int32, (8, LANES), 1)
    where = [(d, half, k) for d in range(chips) for half in range(2) for k in range(groups)]

    for d, half, k in where:
        node = 2 * d + (core if half == 0 else 1 - core)
        at = pl.multiple_of((node * groups + k) * GROUP, GROUP)
        rows = x_ref[0:1, pl.ds(at, GROUP)].astype(jnp.float32).reshape(GROUP_ROWS, LANES)
        scratch[d, half * groups + k] = rows

    def parts_of(d, half, k):
        return [scratch[d, half * groups + k, pl.ds(s, 8, stride=ROWS), :] for s in range(ROWS)]

    tiles = [jnp.zeros((8, LANES), jnp.float32)] * groups
    for d, half, k in where:
        column = lane == half * SEND_LANE + d * groups + k
        tiles[k] = jnp.where(column, peak_of(parts_of(d, half, k)), tiles[k])
    tile = tiles[0]
    for k in range(1, groups):
        tile = jnp.maximum(tile, tiles[k])
    scale, _ = scale_of(tile)
    scale_ref[0] = jnp.where(tile > 0, scale, 0.0)

    for d, half, k in where:
        at = half * SEND_LANE + d * groups + k
        s_col = jnp.broadcast_to(scale[:, at : at + 1], (8, LANES))
        grid, nudge = s_col * (1.5 * 2.0**23), s_col * 2.0**-12
        done = [((part + nudge) + grid) - grid for part in parts_of(d, half, k)]
        o_ref, slot = (send_refs[d % PIECES], d // PIECES) if half else (own_ref, d)
        at = slice(k * GROUP_ROWS, (k + 1) * GROUP_ROWS)
        o_ref[slot, 0, at, :] = jnp.concatenate(done, axis=0).astype(jnp.bfloat16)


def encode_kernel(
    chips, groups, count, own_ref, mine_ref, theirs_ref, before_ref, *refs
):
    *peer_refs, m_ref, flag_ref, buffer, aux, packed, bad, sems, aux_sem = refs
    g = pl.program_id(0)
    slot = lax.rem(g, 2)
    rows = groups * GROUP_ROWS
    lane = lax.broadcasted_iota(jnp.int32, (8, LANES), 1)

    def copy(step, at):
        where = m_ref.at[:, pl.ds(pl.multiple_of(step * rows, rows), rows), :]
        return pltpu.make_async_copy(buffer.at[at], where, sems.at[at])

    @pl.when(g == 0)
    def _():
        bad[...] = before_ref[...]
        packed[...] = jnp.ones_like(packed)

    @pl.when(g >= 2)
    def _():
        copy(g - 2, slot).wait()

    mine, theirs = mine_ref[0], pltpu.roll(theirs_ref[0], SEND_LANE, 1)
    high, low = jnp.maximum(mine, theirs), jnp.minimum(mine, theirs)
    bad[...] = jnp.where((low > 0) & (high > RATIO * low), 1.0, bad[...])
    scale, inverse = scale_of(127.0 * high)
    weight = inverse * (RATIO / STEPS)

    for d in range(chips):
        tile = packed[d]
        for k in range(groups):
            column = slice(d * groups + k, d * groups + k + 1)
            tile = jnp.where(lane == g * groups + k, scale[:, column], tile)
            w_col = jnp.broadcast_to(weight[:, column], (8, LANES))
            at = slice(k * GROUP_ROWS, (k + 1) * GROUP_ROWS)
            peer = peer_refs[d % PIECES][d // PIECES, 0, at, :].astype(jnp.float32)
            total = own_ref[d, 0, at, :].astype(jnp.float32) + peer
            out = []
            for s in range(ROWS):
                part = total[8 * s : 8 * s + 8]
                code = jnp.exp2(jnp.abs(part) * w_col - OFFSET)
                out.append(jnp.where(part < 0, -code, code))
            buffer[slot, d, at, :] = jnp.concatenate(out, axis=0).astype(jnp.bfloat16)
        packed[d] = tile
    copy(g, slot).start()

    @pl.when(g == count - 1)
    def _():
        flag = jnp.max(bad[...])
        flag_ref[...] = bad[...]
        for d in range(chips):
            unit = packed[d] * jnp.where(flag > 0, jnp.float32(jnp.nan), 1.0 / RATIO)
            aux[d] = jnp.concatenate([unit, unit], axis=0).astype(jnp.bfloat16)
        last = pltpu.make_async_copy(aux, m_ref.at[:, pl.ds(count * rows, AUX_ROWS), :], aux_sem)
        last.start()
        last.wait()
        if count >= 2:
            copy(g - 1, 1 - slot).wait()
        copy(g, slot).wait()


def decode_kernel(
    chips, groups, start, final, r_ref, aux_ref, before_ref, o_ref, buffer, units, spoilt, sems, bad
):
    del before_ref
    g, count = pl.program_id(0), pl.num_programs(0)
    slot = lax.rem(g, 2)

    def copy(step, at):
        return pltpu.make_async_copy(buffer.at[at], o_ref.at[step + start], sems.at[at])

    @pl.when(g == 0)
    def _():
        total = jnp.zeros((8, LANES), jnp.float32)
        for d in range(chips):
            units[d] = aux_ref[d].astype(jnp.float32)[0:8]
            total = total + units[d]
        if final:
            spoilt[0] = jnp.max(jnp.where(jnp.isnan(total), 1, 0)).astype(jnp.int32)

    @pl.when(g >= 2)
    def _():
        copy(g - 2, slot).wait()

    rolled = [pltpu.roll(units[d], LANES - g * groups, 1) for d in range(chips)]
    for k in range(groups):
        at = slice(k * GROUP_ROWS, (k + 1) * GROUP_ROWS)
        total = [jnp.zeros((8, LANES), jnp.float32)] * ROWS
        for d in range(chips):
            unit = jnp.broadcast_to(rolled[d][:, k : k + 1], (8, LANES))
            code = r_ref[d, at, :].astype(jnp.float32)
            for s in range(ROWS):
                part = code[8 * s : 8 * s + 8]
                size = jnp.floor(jnp.log2(jnp.abs(part)) * STEPS + (OFFSET * STEPS + 0.5))
                total[s] = total[s] + size * jnp.where(part < 0, -unit, unit)
        buffer[slot, at, :] = jnp.concatenate(requantized(total), axis=0).astype(jnp.bfloat16)
    copy(g, slot).start()

    @pl.when(g == count - 1)
    def _():
        @pl.when(count >= 2)
        def _():
            copy(g - 1, 1 - slot).wait()

        copy(g, slot).wait()
        if final:
            @pl.when(spoilt[0] > 0)
            def _():
                buffer[0] = jnp.full(buffer.shape[1:], jnp.nan, jnp.bfloat16)

                def spoil(j, carry):
                    one = pltpu.make_async_copy(buffer.at[0], o_ref.at[j], bad)
                    one.start()
                    one.wait()
                    return carry

                lax.fori_loop(0, o_ref.shape[0], spoil, 0)


def first_kernel(nodes, groups, after_ref, x_ref, o_ref, scratch):
    del after_ref

    def step(n, carry):
        for k in range(groups):
            at = pl.multiple_of((n * groups + k) * GROUP, GROUP)
            scratch[k] = x_ref[0:1, pl.ds(at, GROUP)].astype(jnp.float32).reshape(GROUP_ROWS, LANES)
        for k in range(groups):
            parts = [scratch[k, pl.ds(s, 8, stride=ROWS), :] for s in range(ROWS)]
            done = jnp.concatenate(requantized(parts), axis=0)
            o_ref[n, 0, k * GROUP_ROWS : (k + 1) * GROUP_ROWS, :] = done.astype(jnp.bfloat16)
        return carry

    lax.fori_loop(0, nodes, step, 0)


def second_kernel(nodes, groups, r_ref, o_ref):
    for k in range(groups):
        rows = slice(k * GROUP_ROWS, (k + 1) * GROUP_ROWS)
        total = r_ref[0, 0, rows, :].astype(jnp.float32)
        for n in range(1, nodes):
            total = total + r_ref[n, 0, rows, :].astype(jnp.float32)
        parts = [total[8 * s : 8 * s + 8] for s in range(ROWS)]
        o_ref[0, rows, :] = jnp.concatenate(requantized(parts), axis=0).astype(jnp.bfloat16)


def update_kernel(replicas, groups, r_ref, p_ref, m_ref, v_ref, po_ref, mo_ref, vo_ref, bad_ref, scratch):
    for k in range(groups):
        rows = slice(k * GROUP_ROWS, (k + 1) * GROUP_ROWS)
        total = r_ref[0, rows, :].astype(jnp.float32)
        for g in range(1, replicas):
            total = total + r_ref[g, rows, :].astype(jnp.float32)
        for s in range(ROWS):
            scratch[pl.ds(k * GROUP_ROWS + s, 8, stride=ROWS), :] = total[8 * s : 8 * s + 8]
    gradient = scratch[...]
    master = p_ref[...]
    moment = 0.9 * m_ref[...] + 0.1 * gradient
    second = 0.95 * v_ref[...] + 0.05 * gradient * gradient
    mo_ref[...] = moment
    vo_ref[...] = second
    po_ref[...] = master - 0.02 * (moment / (jnp.sqrt(second) + 1e-08) + 0.1 * master)
    spoilt = jnp.max(jnp.where(jnp.isnan(gradient[0:8]), 1.0, 0.0))
    bad_ref[0] = jnp.where(spoilt > 0, 1, 0).astype(jnp.int32)


COST = pl.CostEstimate(flops=1, bytes_accessed=1, transcendentals=0)


def quantized(grads, after, start, count, chips, shard):
    rows, groups = shard // LANES, shard // GROUP
    core = lax.axis_index("core").astype(jnp.int32).reshape(1)

    def block(size):
        shape = jax.ShapeDtypeStruct((size, count, rows, LANES), jnp.bfloat16)
        return shape, pl.BlockSpec((size, 1, rows, LANES), lambda g: (0, g, 0, 0))

    blocks = [block(chips)] + [block(chips // PIECES)] * PIECES
    tiles = jax.ShapeDtypeStruct((count, 8, LANES), jnp.float32)
    own, *send, scales = pl.pallas_call(
        lambda *refs: pair_kernel(chips, groups, *refs),
        name="quantize",
        grid=(count,),
        in_specs=[
            pl.BlockSpec(memory_space=pltpu.SMEM),
            pl.BlockSpec((1, 2 * chips * shard), lambda g: (0, g + start)),
            pl.BlockSpec(memory_space=pl.ANY),
        ],
        out_specs=[b for _, b in blocks] + [pl.BlockSpec((1, 8, LANES), lambda g: (g, 0, 0))],
        out_shape=[a for a, _ in blocks] + [tiles],
        scratch_shapes=[pltpu.VMEM((chips, 2 * groups, GROUP_ROWS, LANES), jnp.float32)],
        compiler_params=PARAMS_Q,
        cost_estimate=COST,
    )(core, grads, after)
    peer, peer_scales = jax.tree.map(lambda a: lax.ppermute(a, "core", [(0, 1), (1, 0)]), (send, scales))
    return own, peer, scales, peer_scales


def pair_sums(own, peer, scales, peer_scales, before, after=()):
    chips, count, rows = own.shape[:3]
    half_spec = pl.BlockSpec((chips, 1, rows, LANES), lambda g: (0, g, 0, 0))
    piece_spec = pl.BlockSpec((chips // PIECES, 1, rows, LANES), lambda g: (0, g, 0, 0))
    tile_spec = pl.BlockSpec((1, 8, LANES), lambda g: (g, 0, 0))
    flag = jax.ShapeDtypeStruct((8, LANES), jnp.float32)
    whole = pl.BlockSpec((8, LANES), lambda g: (0, 0))
    return pl.pallas_call(
        lambda *refs: encode_kernel(chips, rows // GROUP_ROWS, count, *refs),
        name="add_and_encode",
        grid=(count,),
        in_specs=[half_spec, tile_spec, tile_spec, whole] + [piece_spec] * PIECES,
        out_specs=[pl.BlockSpec(memory_space=pl.ANY), whole],
        out_shape=[
            jax.ShapeDtypeStruct((chips, count * rows + AUX_ROWS, LANES), jnp.bfloat16), flag,
        ],
        scratch_shapes=[
            pltpu.VMEM((2, chips, rows, LANES), jnp.bfloat16),
            pltpu.VMEM((chips, AUX_ROWS, LANES), jnp.bfloat16),
            pltpu.VMEM((chips, 8, LANES), jnp.float32),
            pltpu.VMEM((8, LANES), jnp.float32),
            pltpu.SemaphoreType.DMA((2,)),
            pltpu.SemaphoreType.DMA,
        ],
        compiler_params=PARAMS_C,
        cost_estimate=COST,
    )(own, scales, peer_scales, before, *peer)


def node_sums(received, partial, start, count, chips, final):
    rows = partial.shape[1]
    return pl.pallas_call(
        lambda *refs: decode_kernel(chips, rows // GROUP_ROWS, start, final, *refs),
        name="decode_and_requantize",
        grid=(count,),
        in_specs=[
            pl.BlockSpec((chips, rows, LANES), lambda g: (0, g, 0)),
            pl.BlockSpec((chips, AUX_ROWS, LANES), lambda g: (0, count * rows // AUX_ROWS, 0)),
            pl.BlockSpec(memory_space=pl.ANY),
        ],
        out_specs=pl.BlockSpec(memory_space=pl.ANY),
        out_shape=jax.ShapeDtypeStruct(partial.shape, partial.dtype),
        scratch_shapes=[
            pltpu.VMEM((2, rows, LANES), jnp.bfloat16),
            pltpu.VMEM((chips, 8, LANES), jnp.float32),
            pltpu.SMEM((1,), jnp.int32),
            pltpu.SemaphoreType.DMA((2,)),
            pltpu.SemaphoreType.DMA,
        ],
        input_output_aliases={2: 0},
        compiler_params=PARAMS,
        cost_estimate=COST,
    )(received, received, partial)


def plain_sums(grads, after, replicas, nodes, shard):
    rows, groups = shard // LANES, shard // GROUP
    first = pl.pallas_call(
        lambda *refs: first_kernel(nodes, groups, *refs),
        name="plain_quantize",
        grid=(replicas,),
        in_specs=[
            pl.BlockSpec(memory_space=pltpu.SMEM),
            pl.BlockSpec((1, nodes * shard), lambda g: (0, g)),
        ],
        out_specs=pl.BlockSpec((nodes, 1, rows, LANES), lambda g: (0, g, 0, 0)),
        out_shape=jax.ShapeDtypeStruct((nodes, replicas, rows, LANES), jnp.bfloat16),
        scratch_shapes=[pltpu.VMEM((groups, GROUP_ROWS, LANES), jnp.float32)],
        compiler_params=PARAMS,
    )(after, grads)
    received = lax.all_to_all(first, ("chip", "core"), split_axis=0, concat_axis=0, tiled=True)
    partial = pl.pallas_call(
        lambda *refs: second_kernel(nodes, groups, *refs),
        name="plain_requantize",
        grid=(replicas,),
        in_specs=[pl.BlockSpec((nodes, 1, rows, LANES), lambda g: (0, g, 0, 0))],
        out_specs=pl.BlockSpec((1, rows, LANES), lambda g: (g, 0, 0)),
        out_shape=jax.ShapeDtypeStruct((replicas, rows, LANES), jnp.bfloat16),
        compiler_params=PARAMS,
    )(received)
    return lax.all_to_all(partial, "group", split_axis=0, concat_axis=0, tiled=True)


def update(owned, master, moment, second):
    replicas, rows = owned.shape[:2]
    state = jax.ShapeDtypeStruct((rows, LANES), jnp.float32)
    whole = pl.BlockSpec(memory_space=pltpu.VMEM)
    return pl.pallas_call(
        lambda *refs: update_kernel(replicas, rows // GROUP_ROWS, *refs),
        name="adamw_update",
        out_shape=(state, state, state, jax.ShapeDtypeStruct((1,), jnp.int32)),
        out_specs=(whole, whole, whole, pl.BlockSpec(memory_space=pltpu.SMEM)),
        scratch_shapes=[pltpu.VMEM((rows, LANES), jnp.float32)],
        compiler_params=PARAMS,
    )(owned, master, moment, second)


def body(grads, master, moment, second):
    replicas = lax.axis_size("group")
    chips = lax.axis_size("chip")
    shard = master.shape[0]
    flag = jnp.zeros((8, LANES), jnp.float32)
    partial = jnp.zeros((replicas, shard // LANES, LANES), jnp.bfloat16)
    start = 0
    for count in PARTS:
        message, flag = pair_sums(*quantized(grads, flag, start, count, chips, shard), flag)
        received = lax.all_to_all(message, "chip", split_axis=0, concat_axis=0, tiled=True)
        partial = node_sums(received, partial, start, count, chips, start + count == replicas)
        start += count
    owned = lax.all_to_all(partial, "group", split_axis=0, concat_axis=0, tiled=True)
    state = [a.reshape(shard // LANES, LANES) for a in (master, moment, second)]

    def general(carry):
        *_, done = update(plain_sums(grads, carry[3], replicas, 2 * chips, shard), *state)
        return (*_, jnp.zeros_like(done))

    *outs, _ = lax.while_loop(lambda carry: carry[3][0] > 0, general, update(owned, *state))
    return tuple(a.reshape(shard) for a in outs)


def solution(mesh):
    groups, nodes = mesh.devices.shape
    cores = Mesh(mesh.devices.reshape(groups, nodes // 2, 2), ("group", "chip", "core"))
    split = P(("group", "chip", "core"))
    in_specs = (P(("group", "chip", "core"), None), split, split, split)
    return jax.shard_map(
        body, mesh=cores, in_specs=in_specs, out_specs=(split, split, split), check_vma=False
    )
```

```python
import jax
import jax.numpy as jnp
from jax import lax
from jax.experimental import pallas as pl
from jax.experimental.pallas import tpu as pltpu
from jax.sharding import Mesh
from jax.sharding import PartitionSpec as P

BLOCK = 512
LANES = 128
ROWS = BLOCK // LANES
GROUP_ROWS = 8 * ROWS
GROUP = GROUP_ROWS * LANES
GROUP_AXES = ("group3", "group2", "group1", "group0")
SEND_LANE = 64
AUX_ROWS = 16

RATIO = 64.0
STEPS = 72.0
OFFSET = 113.0

PARTS = (4, 5, 7)
PIECES = 2
PARAMS = pltpu.CompilerParams(vmem_limit_bytes=48 << 20)
PARAMS_Q = pltpu.CompilerParams(vmem_limit_bytes=48 << 20)
PARAMS_C = pltpu.CompilerParams(vmem_limit_bytes=48 << 20)


def scale_of(peak):
    scale = jnp.full(peak.shape, 2.0**-24, jnp.float32)
    inverse = jnp.full(peak.shape, 2.0**24, jnp.float32)
    for k in (16, 8, 4, 2, 1):
        above = peak > scale * (127.0 * 2.0 ** (k - 1))
        scale = jnp.where(above, scale * 2.0**k, scale)
        inverse = jnp.where(above, inverse * 2.0**-k, inverse)
    return scale, inverse


def peak_of(parts):
    peak = jnp.abs(parts[0])
    for part in parts[1:]:
        peak = jnp.maximum(peak, jnp.abs(part))
    return jnp.max(peak, axis=1, keepdims=True)


def requantized(parts):
    scale, inverse = scale_of(jnp.broadcast_to(peak_of(parts), parts[0].shape))
    return [jnp.floor(part * inverse + 0.5) * scale for part in parts]


def pair_kernel(chips, groups, core_ref, x_ref, after_ref, own_ref, *refs):
    del after_ref
    *send_refs, scale_ref, scratch = refs
    core = core_ref[0]
    lane = lax.broadcasted_iota(jnp.int32, (8, LANES), 1)
    where = [(d, half, k) for d in range(chips) for half in range(2) for k in range(groups)]

    for d, half, k in where:
        node = 2 * d + (core if half == 0 else 1 - core)
        at = pl.multiple_of((node * groups + k) * GROUP, GROUP)
        rows = x_ref[0:1, pl.ds(at, GROUP)].reshape(GROUP_ROWS, LANES)
        scratch[d, half * groups + k] = rows.astype(jnp.float32)

    def parts_of(d, half, k):
        return [scratch[d, half * groups + k, pl.ds(s, 8, stride=ROWS), :] for s in range(ROWS)]

    tiles = [jnp.zeros((8, LANES), jnp.float32)] * groups
    for d, half, k in where:
        column = lane == half * SEND_LANE + d * groups + k
        tiles[k] = jnp.where(column, peak_of(parts_of(d, half, k)), tiles[k])
    tile = tiles[0]
    for k in range(1, groups):
        tile = jnp.maximum(tile, tiles[k])
    scale, _ = scale_of(tile)
    scale_ref[0] = jnp.where(tile > 0, scale, 0.0)

    for d, half, k in where:
        at = half * SEND_LANE + d * groups + k
        s_col = jnp.broadcast_to(scale[:, at : at + 1], (8, LANES))
        grid, nudge = s_col * (1.5 * 2.0**23), s_col * 2.0**-12
        done = [((part + nudge) + grid) - grid for part in parts_of(d, half, k)]
        o_ref, slot = (send_refs[d % PIECES], d // PIECES) if half else (own_ref, d)
        at = slice(k * GROUP_ROWS, (k + 1) * GROUP_ROWS)
        o_ref[slot, 0, at, :] = jnp.concatenate(done, axis=0).astype(jnp.bfloat16)


def encode_kernel(
    chips, groups, count, own_ref, mine_ref, theirs_ref, before_ref, *refs
):
    *peer_refs, m_ref, flag_ref, buffer, aux, packed, bad, sems, aux_sem = refs
    g = pl.program_id(0)
    slot = lax.rem(g, 2)
    rows = groups * GROUP_ROWS
    lane = lax.broadcasted_iota(jnp.int32, (8, LANES), 1)

    def copy(step, at):
        where = m_ref.at[:, pl.ds(pl.multiple_of(step * rows, rows), rows), :]
        return pltpu.make_async_copy(buffer.at[at], where, sems.at[at])

    @pl.when(g == 0)
    def _():
        bad[...] = before_ref[...]
        packed[...] = jnp.ones_like(packed)

    @pl.when(g >= 2)
    def _():
        copy(g - 2, slot).wait()

    mine, theirs = mine_ref[0], pltpu.roll(theirs_ref[0], SEND_LANE, 1)
    high, low = jnp.maximum(mine, theirs), jnp.minimum(mine, theirs)
    bad[...] = jnp.where((low > 0) & (high > RATIO * low), 1.0, bad[...])
    scale, inverse = scale_of(127.0 * high)
    weight = inverse * (RATIO / STEPS)

    for d in range(chips):
        tile = packed[d]
        for k in range(groups):
            column = slice(d * groups + k, d * groups + k + 1)
            tile = jnp.where(lane == g * groups + k, scale[:, column], tile)
            w_col = jnp.broadcast_to(weight[:, column], (8, LANES))
            at = slice(k * GROUP_ROWS, (k + 1) * GROUP_ROWS)
            peer = peer_refs[d % PIECES][d // PIECES, 0, at, :].astype(jnp.float32)
            total = own_ref[d, 0, at, :].astype(jnp.float32) + peer
            out = []
            for s in range(ROWS):
                part = total[8 * s : 8 * s + 8]
                code = jnp.exp2(jnp.abs(part) * w_col - OFFSET)
                out.append(jnp.where(part < 0, -code, code))
            buffer[slot, d, at, :] = jnp.concatenate(out, axis=0).astype(jnp.bfloat16)
        packed[d] = tile
    copy(g, slot).start()

    @pl.when(g == count - 1)
    def _():
        flag = jnp.max(bad[...])
        flag_ref[...] = bad[...]
        for d in range(chips):
            unit = packed[d] * jnp.where(flag > 0, jnp.float32(jnp.nan), 1.0 / RATIO)
            aux[d] = jnp.concatenate([unit, unit], axis=0).astype(jnp.bfloat16)
        last = pltpu.make_async_copy(aux, m_ref.at[:, pl.ds(count * rows, AUX_ROWS), :], aux_sem)
        last.start()
        last.wait()
        if count >= 2:
            copy(g - 1, 1 - slot).wait()
        copy(g, slot).wait()


def slot_of(group):
    slot = 0
    for _ in GROUP_AXES:
        slot = 2 * slot + group % 2
        group = group // 2
    return slot


def partial_sums(chips, groups, g, r_ref, units):
    rolled = [pltpu.roll(units[d], LANES - g * groups, 1) for d in range(chips)]
    for k in range(groups):
        at = slice(k * GROUP_ROWS, (k + 1) * GROUP_ROWS)
        total = [jnp.zeros((8, LANES), jnp.float32)] * ROWS
        for d in range(chips):
            unit = jnp.broadcast_to(rolled[d][:, k : k + 1], (8, LANES))
            code = r_ref[d, at, :].astype(jnp.float32)
            for s in range(ROWS):
                part = code[8 * s : 8 * s + 8]
                size = jnp.floor(jnp.log2(jnp.abs(part)) * STEPS + (OFFSET * STEPS + 0.5))
                total[s] = total[s] + size * jnp.where(part < 0, -unit, unit)
        yield at, jnp.concatenate(requantized(total), axis=0).astype(jnp.bfloat16)


def decode_kernel(chips, groups, r_ref, aux_ref, o_ref, units):
    g = pl.program_id(0)

    @pl.when(g == 0)
    def _():
        for d in range(chips):
            units[d] = aux_ref[d].astype(jnp.float32)[0:8]

    for at, done in partial_sums(chips, groups, g, r_ref, units):
        o_ref[0, at, :] = done


def last_decode_kernel(chips, groups, count, r_ref, aux_ref, *refs):
    *earlier, o_ref, buffer, units, spoilt, sems, early_sems = refs
    g = pl.program_id(0)
    slot = lax.rem(g, 2)
    start = o_ref.shape[0] - count
    blocks = [e.at[i] for e in earlier for i in range(e.shape[0])]

    def copy(step, at):
        return pltpu.make_async_copy(buffer.at[at], o_ref.at[slot_of(step + start)], sems.at[at])

    early = [
        pltpu.make_async_copy(block, o_ref.at[slot_of(i)], early_sems.at[i])
        for i, block in enumerate(blocks)
    ]

    @pl.when(g == 0)
    def _():
        for one in early:
            one.start()
        total = jnp.zeros((8, LANES), jnp.float32)
        for d in range(chips):
            units[d] = aux_ref[d].astype(jnp.float32)[0:8]
            total = total + units[d]
        spoilt[0] = jnp.max(jnp.where(jnp.isnan(total), 1, 0)).astype(jnp.int32)

    @pl.when(g >= 2)
    def _():
        copy(g - 2, slot).wait()

    for at, done in partial_sums(chips, groups, g, r_ref, units):
        buffer[slot, at, :] = done
    copy(g, slot).start()

    @pl.when(g == count - 1)
    def _():
        if count >= 2:
            copy(g - 1, 1 - slot).wait()
        copy(g, slot).wait()
        for one in early:
            one.wait()

        @pl.when(spoilt[0] > 0)
        def _():
            buffer[0] = jnp.full(buffer.shape[1:], jnp.nan, jnp.bfloat16)

            def spoil(j, carry):
                one = pltpu.make_async_copy(buffer.at[0], o_ref.at[j], sems.at[0])
                one.start()
                one.wait()
                return carry

            lax.fori_loop(0, o_ref.shape[0], spoil, 0)


def first_kernel(nodes, groups, after_ref, x_ref, o_ref, scratch):
    del after_ref

    def step(n, carry):
        for k in range(groups):
            at = pl.multiple_of((n * groups + k) * GROUP, GROUP)
            scratch[k] = x_ref[0:1, pl.ds(at, GROUP)].reshape(GROUP_ROWS, LANES).astype(jnp.float32)
        for k in range(groups):
            parts = [scratch[k, pl.ds(s, 8, stride=ROWS), :] for s in range(ROWS)]
            done = jnp.concatenate(requantized(parts), axis=0)
            o_ref[n, 0, k * GROUP_ROWS : (k + 1) * GROUP_ROWS, :] = done.astype(jnp.bfloat16)
        return carry

    lax.fori_loop(0, nodes, step, 0)


def second_kernel(nodes, groups, r_ref, o_ref):
    for k in range(groups):
        rows = slice(k * GROUP_ROWS, (k + 1) * GROUP_ROWS)
        total = r_ref[0, 0, rows, :].astype(jnp.float32)
        for n in range(1, nodes):
            total = total + r_ref[n, 0, rows, :].astype(jnp.float32)
        parts = [total[8 * s : 8 * s + 8] for s in range(ROWS)]
        o_ref[0, rows, :] = jnp.concatenate(requantized(parts), axis=0).astype(jnp.bfloat16)


def update_kernel(replicas, groups, r_ref, p_ref, m_ref, v_ref, po_ref, mo_ref, vo_ref, bad_ref, scratch):
    for k in range(groups):
        rows = slice(k * GROUP_ROWS, (k + 1) * GROUP_ROWS)
        total = r_ref[0, rows, :].astype(jnp.float32)
        for g in range(1, replicas):
            total = total + r_ref[g, rows, :].astype(jnp.float32)
        for s in range(ROWS):
            scratch[pl.ds(k * GROUP_ROWS + s, 8, stride=ROWS), :] = total[8 * s : 8 * s + 8]
    gradient = scratch[...]
    master = p_ref[...]
    moment = 0.9 * m_ref[...] + 0.1 * gradient
    second = 0.95 * v_ref[...] + 0.05 * gradient * gradient
    mo_ref[...] = moment
    vo_ref[...] = second
    po_ref[...] = master - 0.02 * (moment / (jnp.sqrt(second) + 1e-08) + 0.1 * master)
    spoilt = jnp.max(jnp.where(jnp.isnan(gradient[0:8]), 1.0, 0.0))
    bad_ref[0] = jnp.where(spoilt > 0, 1, 0).astype(jnp.int32)


COST = pl.CostEstimate(flops=1, bytes_accessed=1, transcendentals=0)


def quantized(grads, after, start, count, chips, shard):
    rows, groups = shard // LANES, shard // GROUP
    core = lax.axis_index("core").astype(jnp.int32).reshape(1)

    def block(size):
        shape = jax.ShapeDtypeStruct((size, count, rows, LANES), jnp.bfloat16)
        return shape, pl.BlockSpec((size, 1, rows, LANES), lambda g: (0, g, 0, 0))

    blocks = [block(chips)] + [block(chips // PIECES)] * PIECES
    tiles = jax.ShapeDtypeStruct((count, 8, LANES), jnp.float32)
    own, *send, scales = pl.pallas_call(
        lambda *refs: pair_kernel(chips, groups, *refs),
        name="quantize",
        grid=(count,),
        in_specs=[
            pl.BlockSpec(memory_space=pltpu.SMEM),
            pl.BlockSpec((1, 2 * chips * shard), lambda g: (0, g + start)),
            pl.BlockSpec(memory_space=pl.ANY),
        ],
        out_specs=[b for _, b in blocks] + [pl.BlockSpec((1, 8, LANES), lambda g: (g, 0, 0))],
        out_shape=[a for a, _ in blocks] + [tiles],
        scratch_shapes=[pltpu.VMEM((chips, 2 * groups, GROUP_ROWS, LANES), jnp.float32)],
        compiler_params=PARAMS_Q,
        cost_estimate=COST,
    )(core, grads, after)
    peer, peer_scales = jax.tree.map(lambda a: lax.ppermute(a, "core", [(0, 1), (1, 0)]), (send, scales))
    return own, peer, scales, peer_scales


def pair_sums(own, peer, scales, peer_scales, before, after=()):
    chips, count, rows = own.shape[:3]
    half_spec = pl.BlockSpec((chips, 1, rows, LANES), lambda g: (0, g, 0, 0))
    piece_spec = pl.BlockSpec((chips // PIECES, 1, rows, LANES), lambda g: (0, g, 0, 0))
    tile_spec = pl.BlockSpec((1, 8, LANES), lambda g: (g, 0, 0))
    flag = jax.ShapeDtypeStruct((8, LANES), jnp.float32)
    whole = pl.BlockSpec((8, LANES), lambda g: (0, 0))
    return pl.pallas_call(
        lambda *refs: encode_kernel(chips, rows // GROUP_ROWS, count, *refs),
        name="add_and_encode",
        grid=(count,),
        in_specs=[half_spec, tile_spec, tile_spec, whole] + [piece_spec] * PIECES,
        out_specs=[pl.BlockSpec(memory_space=pl.ANY), whole],
        out_shape=[
            jax.ShapeDtypeStruct((chips, count * rows + AUX_ROWS, LANES), jnp.bfloat16), flag,
        ],
        scratch_shapes=[
            pltpu.VMEM((2, chips, rows, LANES), jnp.bfloat16),
            pltpu.VMEM((chips, AUX_ROWS, LANES), jnp.bfloat16),
            pltpu.VMEM((chips, 8, LANES), jnp.float32),
            pltpu.VMEM((8, LANES), jnp.float32),
            pltpu.SemaphoreType.DMA((2,)),
            pltpu.SemaphoreType.DMA,
        ],
        compiler_params=PARAMS_C,
        cost_estimate=COST,
    )(own, scales, peer_scales, before, *peer)


def node_sums(received, count, chips, rows, earlier=None):
    groups = rows // GROUP_ROWS
    in_specs = [
        pl.BlockSpec((chips, rows, LANES), lambda g: (0, g, 0)),
        pl.BlockSpec((chips, AUX_ROWS, LANES), lambda g: (0, count * rows // AUX_ROWS, 0)),
    ]
    units = pltpu.VMEM((chips, 8, LANES), jnp.float32)
    if earlier is None:
        return pl.pallas_call(
            lambda *refs: decode_kernel(chips, groups, *refs),
            name="decode_and_requantize",
            grid=(count,),
            in_specs=in_specs,
            out_specs=pl.BlockSpec((1, rows, LANES), lambda g: (g, 0, 0)),
            out_shape=jax.ShapeDtypeStruct((count, rows, LANES), jnp.bfloat16),
            scratch_shapes=[units],
            compiler_params=PARAMS,
            cost_estimate=COST,
        )(received, received)
    replicas = count + sum(e.shape[0] for e in earlier)
    return pl.pallas_call(
        lambda *refs: last_decode_kernel(chips, groups, count, *refs),
        name="last_decode_and_requantize",
        grid=(count,),
        in_specs=in_specs + [pl.BlockSpec(memory_space=pl.ANY)] * len(earlier),
        out_specs=pl.BlockSpec(memory_space=pl.ANY),
        out_shape=jax.ShapeDtypeStruct((replicas, rows, LANES), jnp.bfloat16),
        scratch_shapes=[
            pltpu.VMEM((2, rows, LANES), jnp.bfloat16),
            units,
            pltpu.SMEM((1,), jnp.int32),
            pltpu.SemaphoreType.DMA((2,)),
            pltpu.SemaphoreType.DMA((replicas - count,)),
        ],
        compiler_params=PARAMS,
        cost_estimate=COST,
    )(received, received, *earlier)


def plain_sums(grads, after, replicas, nodes, shard):
    rows, groups = shard // LANES, shard // GROUP
    first = pl.pallas_call(
        lambda *refs: first_kernel(nodes, groups, *refs),
        name="plain_quantize",
        grid=(replicas,),
        in_specs=[
            pl.BlockSpec(memory_space=pltpu.SMEM),
            pl.BlockSpec((1, nodes * shard), lambda g: (0, g)),
        ],
        out_specs=pl.BlockSpec((nodes, 1, rows, LANES), lambda g: (0, g, 0, 0)),
        out_shape=jax.ShapeDtypeStruct((nodes, replicas, rows, LANES), jnp.bfloat16),
        scratch_shapes=[pltpu.VMEM((groups, GROUP_ROWS, LANES), jnp.float32)],
        compiler_params=PARAMS,
    )(after, grads)
    received = lax.all_to_all(first, ("chip", "core"), split_axis=0, concat_axis=0, tiled=True)
    partial = pl.pallas_call(
        lambda *refs: second_kernel(nodes, groups, *refs),
        name="plain_requantize",
        grid=(replicas,),
        in_specs=[pl.BlockSpec((nodes, 1, rows, LANES), lambda g: (0, g, 0, 0))],
        out_specs=pl.BlockSpec((1, rows, LANES), lambda g: (g, 0, 0)),
        out_shape=jax.ShapeDtypeStruct((replicas, rows, LANES), jnp.bfloat16),
        compiler_params=PARAMS,
    )(received)
    return lax.all_to_all(partial, GROUP_AXES, split_axis=0, concat_axis=0, tiled=True)


def update(owned, master, moment, second):
    replicas, rows = owned.shape[:2]
    state = jax.ShapeDtypeStruct((rows, LANES), jnp.float32)
    whole = pl.BlockSpec(memory_space=pltpu.VMEM)
    return pl.pallas_call(
        lambda *refs: update_kernel(replicas, rows // GROUP_ROWS, *refs),
        name="adamw_update",
        out_shape=(state, state, state, jax.ShapeDtypeStruct((1,), jnp.int32)),
        out_specs=(whole, whole, whole, pl.BlockSpec(memory_space=pltpu.SMEM)),
        scratch_shapes=[pltpu.VMEM((rows, LANES), jnp.float32)],
        compiler_params=PARAMS,
    )(owned, master, moment, second)


def body(grads, master, moment, second):
    replicas = lax.axis_size(GROUP_AXES)
    chips = lax.axis_size("chip")
    shard = master.shape[0]
    flag = jnp.zeros((8, LANES), jnp.float32)
    rows = shard // LANES
    partials, start = [], 0
    for count in PARTS:
        message, flag = pair_sums(*quantized(grads, flag, start, count, chips, shard), flag)
        received = lax.all_to_all(message, "chip", split_axis=0, concat_axis=0, tiled=True)
        start += count
        earlier = partials if start == replicas else None
        partial = node_sums(received, count, chips, rows, earlier)
        partials.append(partial)
    owned = lax.all_to_all(partials[-1], GROUP_AXES[::-1], split_axis=0, concat_axis=0, tiled=True)
    state = [a.reshape(shard // LANES, LANES) for a in (master, moment, second)]

    def general(carry):
        *_, done = update(plain_sums(grads, carry[3], replicas, 2 * chips, shard), *state)
        return (*_, jnp.zeros_like(done))

    *outs, _ = lax.while_loop(lambda carry: carry[3][0] > 0, general, update(owned, *state))
    return tuple(a.reshape(shard) for a in outs)


def solution(mesh):
    nodes = mesh.devices.shape[1]
    axes = (*GROUP_AXES, "chip", "core")
    cores = Mesh(mesh.devices.reshape(*[2] * len(GROUP_AXES), nodes // 2, 2), axes)
    split = P(axes)
    in_specs = (P(axes, None), split, split, split)
    return jax.shard_map(
        body, mesh=cores, in_specs=in_specs, out_specs=(split, split, split), check_vma=False
    )
```

```python
import jax
import jax.numpy as jnp
from jax import lax
from jax.experimental import pallas as pl
from jax.experimental.pallas import tpu as pltpu
from jax.sharding import Mesh
from jax.sharding import PartitionSpec as P

BLOCK = 512
LANES = 128
ROWS = BLOCK // LANES
GROUP_ROWS = 8 * ROWS
GROUP = GROUP_ROWS * LANES
GROUP_AXES = ("group3", "group2", "group1", "group0")
SEND_LANE = 64
AUX_ROWS = 16

RATIO = 64.0
STEPS = 72.0
OFFSET = 113.0

PARTS = (4, 6, 6)
PIECES = 4
SHIFTS = ((0, 0), (0, 1), (1, 0), (1, 1), (2, 0), (2, 1), (3, 0), (3, 1))
PARAMS = pltpu.CompilerParams(vmem_limit_bytes=48 << 20)
PARAMS_Q = pltpu.CompilerParams(vmem_limit_bytes=48 << 20)
PARAMS_C = pltpu.CompilerParams(vmem_limit_bytes=48 << 20)


def scale_of(peak):
    scale = jnp.full(peak.shape, 2.0**-24, jnp.float32)
    inverse = jnp.full(peak.shape, 2.0**24, jnp.float32)
    for k in (16, 8, 4, 2, 1):
        above = peak > scale * (127.0 * 2.0 ** (k - 1))
        scale = jnp.where(above, scale * 2.0**k, scale)
        inverse = jnp.where(above, inverse * 2.0**-k, inverse)
    return scale, inverse


def peak_of(parts):
    peak = jnp.abs(parts[0])
    for part in parts[1:]:
        peak = jnp.maximum(peak, jnp.abs(part))
    return jnp.max(peak, axis=1, keepdims=True)


def requantized(parts):
    scale, inverse = scale_of(jnp.broadcast_to(peak_of(parts), parts[0].shape))
    return [jnp.floor(part * inverse + 0.5) * scale for part in parts]


def pair_kernel(chips, groups, place_ref, x_ref, after_ref, own_ref, *refs):
    del after_ref
    *send_refs, scale_ref, scratch = refs
    core = place_ref[chips]
    lane = lax.broadcasted_iota(jnp.int32, (8, LANES), 1)
    where = [(d, half, k) for d in range(chips) for half in range(2) for k in range(groups)]

    for d, half, k in where:
        node = 2 * place_ref[d] + (core if half == 0 else 1 - core)
        at = pl.multiple_of((node * groups + k) * GROUP, GROUP)
        rows = x_ref[0:1, pl.ds(at, GROUP)].reshape(GROUP_ROWS, LANES)
        scratch[d, half * groups + k] = rows.astype(jnp.float32)

    def parts_of(d, half, k):
        return [scratch[d, half * groups + k, pl.ds(s, 8, stride=ROWS), :] for s in range(ROWS)]

    tiles = [jnp.zeros((8, LANES), jnp.float32)] * groups
    for d, half, k in where:
        column = lane == half * SEND_LANE + d * groups + k
        tiles[k] = jnp.where(column, peak_of(parts_of(d, half, k)), tiles[k])
    tile = tiles[0]
    for k in range(1, groups):
        tile = jnp.maximum(tile, tiles[k])
    scale, _ = scale_of(tile)
    scale_ref[0] = jnp.where(tile > 0, scale, 0.0)

    for d, half, k in where:
        at = half * SEND_LANE + d * groups + k
        s_col = jnp.broadcast_to(scale[:, at : at + 1], (8, LANES))
        grid, nudge = s_col * (1.5 * 2.0**23), s_col * 2.0**-12
        done = [((part + nudge) + grid) - grid for part in parts_of(d, half, k)]
        o_ref, slot = (send_refs[d % PIECES], d // PIECES) if half else (own_ref, d)
        at = slice(k * GROUP_ROWS, (k + 1) * GROUP_ROWS)
        o_ref[slot, 0, at, :] = jnp.concatenate(done, axis=0).astype(jnp.bfloat16)


def encode_kernel(
    chips, groups, count, apart, own_ref, mine_ref, theirs_ref, before_ref, *refs
):
    *refs, flag_ref, buffer, aux, packed, bad, sems, aux_sems = refs
    peer_refs, m_refs = refs[:PIECES], refs[PIECES:]
    g = pl.program_id(0)
    slot = lax.rem(g, 2)
    rows = groups * GROUP_ROWS
    lane = lax.broadcasted_iota(jnp.int32, (8, LANES), 1)

    def copies(source, start, size, sem):
        where = pl.ds(pl.multiple_of(start, AUX_ROWS), size)
        if not apart:
            return [pltpu.make_async_copy(source, m_refs[0].at[:, where, :], sem.at[0])]
        return [
            pltpu.make_async_copy(source.at[d], m_refs[d].at[where, :], sem.at[d])
            for d in range(chips)
        ]

    def copy(step, at):
        return copies(buffer.at[at], step * rows, rows, sems.at[at])

    def start(several):
        for one in several:
            one.start()

    def wait(several):
        for one in several:
            one.wait()

    @pl.when(g == 0)
    def _():
        bad[...] = before_ref[...]
        packed[...] = jnp.ones_like(packed)

    @pl.when(g >= 2)
    def _():
        wait(copy(g - 2, slot))

    mine, theirs = mine_ref[0], pltpu.roll(theirs_ref[0], SEND_LANE, 1)
    high, low = jnp.maximum(mine, theirs), jnp.minimum(mine, theirs)
    bad[...] = jnp.where((low > 0) & (high > RATIO * low), 1.0, bad[...])
    scale, inverse = scale_of(127.0 * high)
    weight = inverse * (RATIO / STEPS)

    for d in range(chips):
        tile = packed[d]
        for k in range(groups):
            column = slice(d * groups + k, d * groups + k + 1)
            tile = jnp.where(lane == g * groups + k, scale[:, column], tile)
            w_col = jnp.broadcast_to(weight[:, column], (8, LANES))
            at = slice(k * GROUP_ROWS, (k + 1) * GROUP_ROWS)
            peer = peer_refs[d % PIECES][d // PIECES, 0, at, :].astype(jnp.float32)
            total = own_ref[d, 0, at, :].astype(jnp.float32) + peer
            out = []
            for s in range(ROWS):
                part = total[8 * s : 8 * s + 8]
                code = jnp.exp2(jnp.abs(part) * w_col - OFFSET)
                out.append(jnp.where(part < 0, -code, code))
            buffer[slot, d, at, :] = jnp.concatenate(out, axis=0).astype(jnp.bfloat16)
        packed[d] = tile
    start(copy(g, slot))

    @pl.when(g == count - 1)
    def _():
        flag = jnp.max(bad[...])
        flag_ref[...] = bad[...]
        for d in range(chips):
            unit = packed[d] * jnp.where(flag > 0, jnp.float32(jnp.nan), 1.0 / RATIO)
            aux[d] = jnp.concatenate([unit, unit], axis=0).astype(jnp.bfloat16)
        last = copies(aux, count * rows, AUX_ROWS, aux_sems)
        start(last)
        wait(last)
        if count >= 2:
            wait(copy(g - 1, 1 - slot))
        wait(copy(g, slot))


def slot_of(group):
    slot = 0
    for _ in GROUP_AXES:
        slot = 2 * slot + group % 2
        group = group // 2
    return slot


def partial_sums(chips, groups, g, r_refs, units):
    rolled = [pltpu.roll(units[d], LANES - g * groups, 1) for d in range(chips)]
    for k in range(groups):
        at = slice(k * GROUP_ROWS, (k + 1) * GROUP_ROWS)
        total = [jnp.zeros((8, LANES), jnp.float32)] * ROWS
        for d in range(chips):
            unit = jnp.broadcast_to(rolled[d][:, k : k + 1], (8, LANES))
            code = r_refs[d][at, :].astype(jnp.float32)
            for s in range(ROWS):
                part = code[8 * s : 8 * s + 8]
                size = jnp.floor(jnp.log2(jnp.abs(part)) * STEPS + (OFFSET * STEPS + 0.5))
                total[s] = total[s] + size * jnp.where(part < 0, -unit, unit)
        yield at, jnp.concatenate(requantized(total), axis=0).astype(jnp.bfloat16)


def decode_kernel(chips, groups, r_ref, aux_ref, o_ref, units):
    g = pl.program_id(0)

    @pl.when(g == 0)
    def _():
        for d in range(chips):
            units[d] = aux_ref[d].astype(jnp.float32)[0:8]

    codes = [r_ref.at[d] for d in range(chips)]
    for at, done in partial_sums(chips, groups, g, codes, units):
        o_ref[0, at, :] = done


def last_decode_kernel(chips, groups, count, *refs):
    r_refs, aux_refs, refs = refs[:chips], refs[chips : 2 * chips], refs[2 * chips :]
    *earlier, o_ref, buffer, units, spoilt, sems, early_sems = refs
    g = pl.program_id(0)
    slot = lax.rem(g, 2)
    start = o_ref.shape[0] - count
    blocks = [e.at[i] for e in earlier for i in range(e.shape[0])]

    def copy(step, at):
        return pltpu.make_async_copy(buffer.at[at], o_ref.at[slot_of(step + start)], sems.at[at])

    early = [
        pltpu.make_async_copy(block, o_ref.at[slot_of(i)], early_sems.at[i])
        for i, block in enumerate(blocks)
    ]

    @pl.when(g == 0)
    def _():
        for one in early:
            one.start()
        total = jnp.zeros((8, LANES), jnp.float32)
        for d in range(chips):
            units[d] = aux_refs[d][...].astype(jnp.float32)[0:8]
            total = total + units[d]
        spoilt[0] = jnp.max(jnp.where(jnp.isnan(total), 1, 0)).astype(jnp.int32)

    @pl.when(g >= 2)
    def _():
        copy(g - 2, slot).wait()

    for at, done in partial_sums(chips, groups, g, r_refs, units):
        buffer[slot, at, :] = done
    copy(g, slot).start()

    @pl.when(g == count - 1)
    def _():
        if count >= 2:
            copy(g - 1, 1 - slot).wait()
        copy(g, slot).wait()
        for one in early:
            one.wait()

        @pl.when(spoilt[0] > 0)
        def _():
            buffer[0] = jnp.full(buffer.shape[1:], jnp.nan, jnp.bfloat16)

            def spoil(j, carry):
                one = pltpu.make_async_copy(buffer.at[0], o_ref.at[j], sems.at[0])
                one.start()
                one.wait()
                return carry

            lax.fori_loop(0, o_ref.shape[0], spoil, 0)


def first_kernel(nodes, groups, after_ref, x_ref, o_ref, scratch):
    del after_ref

    def step(n, carry):
        for k in range(groups):
            at = pl.multiple_of((n * groups + k) * GROUP, GROUP)
            scratch[k] = x_ref[0:1, pl.ds(at, GROUP)].reshape(GROUP_ROWS, LANES).astype(jnp.float32)
        for k in range(groups):
            parts = [scratch[k, pl.ds(s, 8, stride=ROWS), :] for s in range(ROWS)]
            done = jnp.concatenate(requantized(parts), axis=0)
            o_ref[n, 0, k * GROUP_ROWS : (k + 1) * GROUP_ROWS, :] = done.astype(jnp.bfloat16)
        return carry

    lax.fori_loop(0, nodes, step, 0)


def second_kernel(nodes, groups, r_ref, o_ref):
    for k in range(groups):
        rows = slice(k * GROUP_ROWS, (k + 1) * GROUP_ROWS)
        total = r_ref[0, 0, rows, :].astype(jnp.float32)
        for n in range(1, nodes):
            total = total + r_ref[n, 0, rows, :].astype(jnp.float32)
        parts = [total[8 * s : 8 * s + 8] for s in range(ROWS)]
        o_ref[0, rows, :] = jnp.concatenate(requantized(parts), axis=0).astype(jnp.bfloat16)


def update_kernel(replicas, groups, r_ref, p_ref, m_ref, v_ref, po_ref, mo_ref, vo_ref, bad_ref, scratch):
    for k in range(groups):
        rows = slice(k * GROUP_ROWS, (k + 1) * GROUP_ROWS)
        total = r_ref[0, rows, :].astype(jnp.float32)
        for g in range(1, replicas):
            total = total + r_ref[g, rows, :].astype(jnp.float32)
        for s in range(ROWS):
            scratch[pl.ds(k * GROUP_ROWS + s, 8, stride=ROWS), :] = total[8 * s : 8 * s + 8]
    gradient = scratch[...]
    master = p_ref[...]
    moment = 0.9 * m_ref[...] + 0.1 * gradient
    second = 0.95 * v_ref[...] + 0.05 * gradient * gradient
    mo_ref[...] = moment
    vo_ref[...] = second
    po_ref[...] = master - 0.02 * (moment / (jnp.sqrt(second) + 1e-08) + 0.1 * master)
    spoilt = jnp.max(jnp.where(jnp.isnan(gradient[0:8]), 1.0, 0.0))
    bad_ref[0] = jnp.where(spoilt > 0, 1, 0).astype(jnp.int32)


COST = pl.CostEstimate(flops=1, bytes_accessed=1, transcendentals=0)


def other_chip(chip, k):
    x, y = chip // 2, chip % 2
    return (x + SHIFTS[k][0]) % 4 * 2 + (y + SHIFTS[k][1]) % 2


def quantized(grads, after, start, count, chips, shard, relative=False):
    rows, groups = shard // LANES, shard // GROUP
    chip = lax.axis_index("chip")
    slots = [other_chip(chip, k) if relative else k for k in range(chips)]
    place = jnp.stack([jnp.asarray(a, jnp.int32) for a in (*slots, lax.axis_index("core"))])

    def block(size):
        shape = jax.ShapeDtypeStruct((size, count, rows, LANES), jnp.bfloat16)
        return shape, pl.BlockSpec((size, 1, rows, LANES), lambda g: (0, g, 0, 0))

    blocks = [block(chips)] + [block(chips // PIECES)] * PIECES
    tiles = jax.ShapeDtypeStruct((count, 8, LANES), jnp.float32)
    own, *send, scales = pl.pallas_call(
        lambda *refs: pair_kernel(chips, groups, *refs),
        name="quantize",
        grid=(count,),
        in_specs=[
            pl.BlockSpec(memory_space=pltpu.SMEM),
            pl.BlockSpec((1, 2 * chips * shard), lambda g: (0, g + start)),
            pl.BlockSpec(memory_space=pl.ANY),
        ],
        out_specs=[b for _, b in blocks] + [pl.BlockSpec((1, 8, LANES), lambda g: (g, 0, 0))],
        out_shape=[a for a, _ in blocks] + [tiles],
        scratch_shapes=[pltpu.VMEM((chips, 2 * groups, GROUP_ROWS, LANES), jnp.float32)],
        compiler_params=PARAMS_Q,
        cost_estimate=COST,
    )(place, grads, after)
    peer, peer_scales = jax.tree.map(lambda a: lax.ppermute(a, "core", [(0, 1), (1, 0)]), (send, scales))
    return own, peer, scales, peer_scales


def pair_sums(own, peer, scales, peer_scales, before, apart=False):
    chips, count, rows = own.shape[:3]
    half_spec = pl.BlockSpec((chips, 1, rows, LANES), lambda g: (0, g, 0, 0))
    piece_spec = pl.BlockSpec((chips // PIECES, 1, rows, LANES), lambda g: (0, g, 0, 0))
    tile_spec = pl.BlockSpec((1, 8, LANES), lambda g: (g, 0, 0))
    flag = jax.ShapeDtypeStruct((8, LANES), jnp.float32)
    whole = pl.BlockSpec((8, LANES), lambda g: (0, 0))
    length, copies = count * rows + AUX_ROWS, chips if apart else 1
    message = jax.ShapeDtypeStruct((length, LANES) if apart else (chips, length, LANES), jnp.bfloat16)
    *messages, flag = pl.pallas_call(
        lambda *refs: encode_kernel(chips, rows // GROUP_ROWS, count, apart, *refs),
        name="add_and_encode",
        grid=(count,),
        in_specs=[half_spec, tile_spec, tile_spec, whole] + [piece_spec] * PIECES,
        out_specs=[pl.BlockSpec(memory_space=pl.ANY)] * copies + [whole],
        out_shape=[message] * copies + [flag],
        scratch_shapes=[
            pltpu.VMEM((2, chips, rows, LANES), jnp.bfloat16),
            pltpu.VMEM((chips, AUX_ROWS, LANES), jnp.bfloat16),
            pltpu.VMEM((chips, 8, LANES), jnp.float32),
            pltpu.VMEM((8, LANES), jnp.float32),
            pltpu.SemaphoreType.DMA((2, copies)),
            pltpu.SemaphoreType.DMA((copies,)),
        ],
        compiler_params=PARAMS_C,
        cost_estimate=COST,
    )(own, scales, peer_scales, before, *peer)
    return messages, flag


def node_sums(received, count, chips, rows, earlier=None):
    groups = rows // GROUP_ROWS
    in_specs = [
        pl.BlockSpec((chips, rows, LANES), lambda g: (0, g, 0)),
        pl.BlockSpec((chips, AUX_ROWS, LANES), lambda g: (0, count * rows // AUX_ROWS, 0)),
    ]
    units = pltpu.VMEM((chips, 8, LANES), jnp.float32)
    if earlier is None:
        return pl.pallas_call(
            lambda *refs: decode_kernel(chips, groups, *refs),
            name="decode_and_requantize",
            grid=(count,),
            in_specs=in_specs,
            out_specs=pl.BlockSpec((1, rows, LANES), lambda g: (g, 0, 0)),
            out_shape=jax.ShapeDtypeStruct((count, rows, LANES), jnp.bfloat16),
            scratch_shapes=[units],
            compiler_params=PARAMS,
            cost_estimate=COST,
        )(received, received)
    replicas = count + sum(e.shape[0] for e in earlier)
    return pl.pallas_call(
        lambda *refs: last_decode_kernel(chips, groups, count, *refs),
        name="last_decode_and_requantize",
        grid=(count,),
        in_specs=[pl.BlockSpec((rows, LANES), lambda g: (g, 0))] * chips
        + [pl.BlockSpec((AUX_ROWS, LANES), lambda g: (count * rows // AUX_ROWS, 0))] * chips
        + [pl.BlockSpec(memory_space=pl.ANY)] * len(earlier),
        out_specs=pl.BlockSpec(memory_space=pl.ANY),
        out_shape=jax.ShapeDtypeStruct((replicas, rows, LANES), jnp.bfloat16),
        scratch_shapes=[
            pltpu.VMEM((2, rows, LANES), jnp.bfloat16),
            units,
            pltpu.SMEM((1,), jnp.int32),
            pltpu.SemaphoreType.DMA((2,)),
            pltpu.SemaphoreType.DMA((replicas - count,)),
        ],
        compiler_params=PARAMS,
        cost_estimate=COST,
    )(*received, *received, *earlier)


def plain_sums(grads, after, replicas, nodes, shard):
    rows, groups = shard // LANES, shard // GROUP
    first = pl.pallas_call(
        lambda *refs: first_kernel(nodes, groups, *refs),
        name="plain_quantize",
        grid=(replicas,),
        in_specs=[
            pl.BlockSpec(memory_space=pltpu.SMEM),
            pl.BlockSpec((1, nodes * shard), lambda g: (0, g)),
        ],
        out_specs=pl.BlockSpec((nodes, 1, rows, LANES), lambda g: (0, g, 0, 0)),
        out_shape=jax.ShapeDtypeStruct((nodes, replicas, rows, LANES), jnp.bfloat16),
        scratch_shapes=[pltpu.VMEM((groups, GROUP_ROWS, LANES), jnp.float32)],
        compiler_params=PARAMS,
    )(after, grads)
    received = lax.all_to_all(first, ("chip", "core"), split_axis=0, concat_axis=0, tiled=True)
    partial = pl.pallas_call(
        lambda *refs: second_kernel(nodes, groups, *refs),
        name="plain_requantize",
        grid=(replicas,),
        in_specs=[pl.BlockSpec((nodes, 1, rows, LANES), lambda g: (0, g, 0, 0))],
        out_specs=pl.BlockSpec((1, rows, LANES), lambda g: (g, 0, 0)),
        out_shape=jax.ShapeDtypeStruct((replicas, rows, LANES), jnp.bfloat16),
        compiler_params=PARAMS,
    )(received)
    return lax.all_to_all(partial, GROUP_AXES, split_axis=0, concat_axis=0, tiled=True)


def update(owned, master, moment, second):
    replicas, rows = owned.shape[:2]
    state = jax.ShapeDtypeStruct((rows, LANES), jnp.float32)
    whole = pl.BlockSpec(memory_space=pltpu.VMEM)
    return pl.pallas_call(
        lambda *refs: update_kernel(replicas, rows // GROUP_ROWS, *refs),
        name="adamw_update",
        out_shape=(state, state, state, jax.ShapeDtypeStruct((1,), jnp.int32)),
        out_specs=(whole, whole, whole, pl.BlockSpec(memory_space=pltpu.SMEM)),
        scratch_shapes=[pltpu.VMEM((rows, LANES), jnp.float32)],
        compiler_params=PARAMS,
    )(owned, master, moment, second)


def body(grads, master, moment, second):
    replicas = lax.axis_size(GROUP_AXES)
    chips = lax.axis_size("chip")
    shard = master.shape[0]
    flag = jnp.zeros((8, LANES), jnp.float32)
    rows = shard // LANES
    partials, start = [], 0
    for count in PARTS:
        last = start + count == replicas
        ready = quantized(grads, flag, start, count, chips, shard, last)
        messages, flag = pair_sums(*ready, flag, last)
        if last:
            received = [
                lax.ppermute(m, "chip", [(c, other_chip(c, k)) for c in range(chips)]) if k else m
                for k, m in enumerate(messages)
            ]
        else:
            received = lax.all_to_all(messages[0], "chip", split_axis=0, concat_axis=0, tiled=True)
        partials.append(node_sums(received, count, chips, rows, partials if last else None))
        start += count
    owned = lax.all_to_all(partials[-1], GROUP_AXES[::-1], split_axis=0, concat_axis=0, tiled=True)
    state = [a.reshape(shard // LANES, LANES) for a in (master, moment, second)]

    def general(carry):
        *_, done = update(plain_sums(grads, carry[3], replicas, 2 * chips, shard), *state)
        return (*_, jnp.zeros_like(done))

    *outs, _ = lax.while_loop(lambda carry: carry[3][0] > 0, general, update(owned, *state))
    return tuple(a.reshape(shard) for a in outs)


def solution(mesh):
    nodes = mesh.devices.shape[1]
    axes = (*GROUP_AXES, "chip", "core")
    cores = Mesh(mesh.devices.reshape(*[2] * len(GROUP_AXES), nodes // 2, 2), axes)
    split = P(axes)
    in_specs = (P(axes, None), split, split, split)
    return jax.shard_map(
        body, mesh=cores, in_specs=in_specs, out_specs=(split, split, split), check_vma=False
    )
```

```python
import jax
import jax.numpy as jnp
from jax import lax
from jax.experimental import pallas as pl
from jax.experimental.pallas import tpu as pltpu
from jax.sharding import Mesh
from jax.sharding import PartitionSpec as P

BLOCK = 512
LANES = 128
ROWS = BLOCK // LANES
GROUP_ROWS = 8 * ROWS
GROUP = GROUP_ROWS * LANES
GROUP_AXES = ("group3", "group2", "group1", "group0")
SEND_LANE = 64
AUX_ROWS = 16

RATIO = 64.0
STEPS = 72.0
OFFSET = 113.0

PARTS = (4, 6, 6)
PIECES = 4
SHIFTS = ((0, 0), (0, 1), (1, 0), (1, 1), (2, 0), (2, 1), (3, 0), (3, 1))
PARAMS = pltpu.CompilerParams(vmem_limit_bytes=48 << 20)
PARAMS_Q = pltpu.CompilerParams(vmem_limit_bytes=48 << 20)
PARAMS_C = pltpu.CompilerParams(vmem_limit_bytes=48 << 20)


def scale_of(peak):
    scale = jnp.full(peak.shape, 2.0**-24, jnp.float32)
    inverse = jnp.full(peak.shape, 2.0**24, jnp.float32)
    for k in (16, 8, 4, 2, 1):
        above = peak > scale * (127.0 * 2.0 ** (k - 1))
        scale = jnp.where(above, scale * 2.0**k, scale)
        inverse = jnp.where(above, inverse * 2.0**-k, inverse)
    return scale, inverse


def peak_of(parts):
    peak = jnp.abs(parts[0])
    for part in parts[1:]:
        peak = jnp.maximum(peak, jnp.abs(part))
    return jnp.max(peak, axis=1, keepdims=True)


def requantized(parts):
    scale, inverse = scale_of(jnp.broadcast_to(peak_of(parts), parts[0].shape))
    return [jnp.floor(part * inverse + 0.5) * scale for part in parts]


def pair_kernel(chips, groups, place_ref, x_ref, after_ref, own_ref, *refs):
    del after_ref
    *send_refs, scale_ref, scratch = refs
    core = place_ref[chips]
    lane = lax.broadcasted_iota(jnp.int32, (8, LANES), 1)
    where = [(d, half, k) for d in range(chips) for half in range(2) for k in range(groups)]

    for d, half, k in where:
        node = 2 * place_ref[d] + (core if half == 0 else 1 - core)
        at = pl.multiple_of((node * groups + k) * GROUP, GROUP)
        rows = x_ref[0:1, pl.ds(at, GROUP)].reshape(GROUP_ROWS, LANES)
        scratch[d, half * groups + k] = rows.astype(jnp.float32)

    def parts_of(d, half, k):
        return [scratch[d, half * groups + k, pl.ds(s, 8, stride=ROWS), :] for s in range(ROWS)]

    tiles = [jnp.zeros((8, LANES), jnp.float32)] * groups
    for d, half, k in where:
        column = lane == half * SEND_LANE + d * groups + k
        tiles[k] = jnp.where(column, peak_of(parts_of(d, half, k)), tiles[k])
    tile = tiles[0]
    for k in range(1, groups):
        tile = jnp.maximum(tile, tiles[k])
    scale, _ = scale_of(tile)
    scale_ref[0] = jnp.where(tile > 0, scale, 0.0)

    for d, half, k in where:
        at = half * SEND_LANE + d * groups + k
        s_col = jnp.broadcast_to(scale[:, at : at + 1], (8, LANES))
        grid, nudge = s_col * (1.5 * 2.0**23), s_col * 2.0**-12
        done = [((part + nudge) + grid) - grid for part in parts_of(d, half, k)]
        o_ref, slot = (send_refs[d % PIECES], d // PIECES) if half else (own_ref, d)
        at = slice(k * GROUP_ROWS, (k + 1) * GROUP_ROWS)
        o_ref[slot, 0, at, :] = jnp.concatenate(done, axis=0).astype(jnp.bfloat16)


def encode_kernel(
    chips, groups, count, apart, own_ref, mine_ref, theirs_ref, before_ref, *refs
):
    *refs, flag_ref, buffer, aux, packed, bad, sems, aux_sems = refs
    peer_refs, m_refs = refs[:PIECES], refs[PIECES:]
    g = pl.program_id(0)
    slot = lax.rem(g, 2)
    rows = groups * GROUP_ROWS
    lane = lax.broadcasted_iota(jnp.int32, (8, LANES), 1)

    def copies(source, start, size, sem):
        where = pl.ds(pl.multiple_of(start, AUX_ROWS), size)
        if not apart:
            return [pltpu.make_async_copy(source, m_refs[0].at[:, where, :], sem.at[0])]
        return [
            pltpu.make_async_copy(source.at[d], m_refs[d].at[where, :], sem.at[d])
            for d in range(chips)
        ]

    def copy(step, at):
        return copies(buffer.at[at], step * rows, rows, sems.at[at])

    def start(several):
        for one in several:
            one.start()

    def wait(several):
        for one in several:
            one.wait()

    @pl.when(g == 0)
    def _():
        bad[...] = before_ref[...]
        packed[...] = jnp.ones_like(packed)

    @pl.when(g >= 2)
    def _():
        wait(copy(g - 2, slot))

    mine, theirs = mine_ref[0], pltpu.roll(theirs_ref[0], SEND_LANE, 1)
    high, low = jnp.maximum(mine, theirs), jnp.minimum(mine, theirs)
    bad[...] = jnp.where((low > 0) & (high > RATIO * low), 1.0, bad[...])
    scale, inverse = scale_of(127.0 * high)
    weight = inverse * (RATIO / STEPS)

    for d in range(chips):
        tile = packed[d]
        for k in range(groups):
            column = slice(d * groups + k, d * groups + k + 1)
            tile = jnp.where(lane == g * groups + k, scale[:, column], tile)
            w_col = jnp.broadcast_to(weight[:, column], (8, LANES))
            at = slice(k * GROUP_ROWS, (k + 1) * GROUP_ROWS)
            peer = peer_refs[d % PIECES][d // PIECES, 0, at, :].astype(jnp.float32)
            total = own_ref[d, 0, at, :].astype(jnp.float32) + peer
            out = []
            for s in range(ROWS):
                part = total[8 * s : 8 * s + 8]
                code = jnp.exp2(jnp.abs(part) * w_col - OFFSET)
                out.append(jnp.where(part < 0, -code, code))
            buffer[slot, d, at, :] = jnp.concatenate(out, axis=0).astype(jnp.bfloat16)
        packed[d] = tile
    start(copy(g, slot))

    @pl.when(g == count - 1)
    def _():
        flag = jnp.max(bad[...])
        flag_ref[...] = bad[...]
        for d in range(chips):
            unit = packed[d] * jnp.where(flag > 0, jnp.float32(jnp.nan), 1.0 / RATIO)
            aux[d] = jnp.concatenate([unit, unit], axis=0).astype(jnp.bfloat16)
        last = copies(aux, count * rows, AUX_ROWS, aux_sems)
        start(last)
        wait(last)
        if count >= 2:
            wait(copy(g - 1, 1 - slot))
        wait(copy(g, slot))


def slot_of(group):
    slot = 0
    for _ in GROUP_AXES:
        slot = 2 * slot + group % 2
        group = group // 2
    return slot


def partial_sums(chips, groups, g, r_refs, units, first=0):
    rolled = [pltpu.roll(units[d], LANES - g * groups, 1) for d in range(chips)]
    for k in range(groups):
        at = slice(k * GROUP_ROWS, (k + 1) * GROUP_ROWS)
        total = [jnp.zeros((8, LANES), jnp.float32)] * ROWS
        for d in range(chips):
            unit = jnp.broadcast_to(rolled[d][:, k : k + 1], (8, LANES))
            code = r_refs[d][first + at.start : first + at.stop, :].astype(jnp.float32)
            for s in range(ROWS):
                part = code[8 * s : 8 * s + 8]
                size = jnp.floor(jnp.log2(jnp.abs(part)) * STEPS + (OFFSET * STEPS + 0.5))
                total[s] = total[s] + size * jnp.where(part < 0, -unit, unit)
        yield at, jnp.concatenate(requantized(total), axis=0).astype(jnp.bfloat16)


def decode_kernel(chips, groups, r_ref, aux_ref, o_ref, units):
    g = pl.program_id(0)

    @pl.when(g == 0)
    def _():
        for d in range(chips):
            units[d] = aux_ref[d].astype(jnp.float32)[0:8]

    codes = [r_ref.at[d] for d in range(chips)]
    for at, done in partial_sums(chips, groups, g, codes, units):
        o_ref[0, at, :] = done


def last_decode_kernel(chips, groups, count, each, *refs):
    r_refs, aux_refs, refs = refs[:chips], refs[chips : 2 * chips], refs[2 * chips :]
    *earlier, o_ref, buffer, units, spoilt, sems, early_sems = refs
    g = pl.program_id(0)
    slot = lax.rem(g, 2)
    start = o_ref.shape[0] - count
    blocks = [e.at[i] for e in earlier for i in range(e.shape[0])]

    steps = count // each

    def copy(step, at):
        return [
            pltpu.make_async_copy(
                buffer.at[at, e], o_ref.at[slot_of(step * each + e + start)], sems.at[at, e]
            )
            for e in range(each)
        ]

    def wait(several):
        for one in several:
            one.wait()

    early = [
        pltpu.make_async_copy(block, o_ref.at[slot_of(i)], early_sems.at[i])
        for i, block in enumerate(blocks)
    ]

    @pl.when(g == 0)
    def _():
        for one in early:
            one.start()
        total = jnp.zeros((8, LANES), jnp.float32)
        for d in range(chips):
            units[d] = aux_refs[d][...].astype(jnp.float32)[0:8]
            total = total + units[d]
        spoilt[0] = jnp.max(jnp.where(jnp.isnan(total), 1, 0)).astype(jnp.int32)

    @pl.when(g >= 2)
    def _():
        wait(copy(g - 2, slot))

    rows = groups * GROUP_ROWS
    for e in range(each):
        for at, done in partial_sums(chips, groups, g * each + e, r_refs, units, e * rows):
            buffer[slot, e, at, :] = done
        copy(g, slot)[e].start()

    @pl.when(g == steps - 1)
    def _():
        if steps >= 2:
            wait(copy(g - 1, 1 - slot))
        wait(copy(g, slot))
        for one in early:
            one.wait()

        @pl.when(spoilt[0] > 0)
        def _():
            buffer[0, 0] = jnp.full(buffer.shape[2:], jnp.nan, jnp.bfloat16)

            def spoil(j, carry):
                one = pltpu.make_async_copy(buffer.at[0, 0], o_ref.at[j], sems.at[0, 0])
                one.start()
                one.wait()
                return carry

            lax.fori_loop(0, o_ref.shape[0], spoil, 0)


def first_kernel(nodes, groups, after_ref, x_ref, o_ref, scratch):
    del after_ref

    def step(n, carry):
        for k in range(groups):
            at = pl.multiple_of((n * groups + k) * GROUP, GROUP)
            scratch[k] = x_ref[0:1, pl.ds(at, GROUP)].reshape(GROUP_ROWS, LANES).astype(jnp.float32)
        for k in range(groups):
            parts = [scratch[k, pl.ds(s, 8, stride=ROWS), :] for s in range(ROWS)]
            done = jnp.concatenate(requantized(parts), axis=0)
            o_ref[n, 0, k * GROUP_ROWS : (k + 1) * GROUP_ROWS, :] = done.astype(jnp.bfloat16)
        return carry

    lax.fori_loop(0, nodes, step, 0)


def second_kernel(nodes, groups, r_ref, o_ref):
    for k in range(groups):
        rows = slice(k * GROUP_ROWS, (k + 1) * GROUP_ROWS)
        total = r_ref[0, 0, rows, :].astype(jnp.float32)
        for n in range(1, nodes):
            total = total + r_ref[n, 0, rows, :].astype(jnp.float32)
        parts = [total[8 * s : 8 * s + 8] for s in range(ROWS)]
        o_ref[0, rows, :] = jnp.concatenate(requantized(parts), axis=0).astype(jnp.bfloat16)


def update_kernel(replicas, groups, r_ref, p_ref, m_ref, v_ref, po_ref, mo_ref, vo_ref, bad_ref, scratch):
    for k in range(groups):
        rows = slice(k * GROUP_ROWS, (k + 1) * GROUP_ROWS)
        total = r_ref[0, rows, :].astype(jnp.float32)
        for g in range(1, replicas):
            total = total + r_ref[g, rows, :].astype(jnp.float32)
        for s in range(ROWS):
            scratch[pl.ds(k * GROUP_ROWS + s, 8, stride=ROWS), :] = total[8 * s : 8 * s + 8]
    gradient = scratch[...]
    master = p_ref[...]
    moment = 0.9 * m_ref[...] + 0.1 * gradient
    second = 0.95 * v_ref[...] + 0.05 * gradient * gradient
    mo_ref[...] = moment
    vo_ref[...] = second
    po_ref[...] = master - 0.02 * (moment / (jnp.sqrt(second) + 1e-08) + 0.1 * master)
    spoilt = jnp.max(jnp.where(jnp.isnan(gradient[0:8]), 1.0, 0.0))
    bad_ref[0] = jnp.where(spoilt > 0, 1, 0).astype(jnp.int32)


COST = pl.CostEstimate(flops=1, bytes_accessed=1, transcendentals=0)


def other_chip(chip, k):
    x, y = chip // 2, chip % 2
    return (x + SHIFTS[k][0]) % 4 * 2 + (y + SHIFTS[k][1]) % 2


def quantized(grads, after, start, count, chips, shard, relative=False):
    rows, groups = shard // LANES, shard // GROUP
    chip = lax.axis_index("chip")
    slots = [other_chip(chip, k) if relative else k for k in range(chips)]
    place = jnp.stack([jnp.asarray(a, jnp.int32) for a in (*slots, lax.axis_index("core"))])

    def block(size):
        shape = jax.ShapeDtypeStruct((size, count, rows, LANES), jnp.bfloat16)
        return shape, pl.BlockSpec((size, 1, rows, LANES), lambda g: (0, g, 0, 0))

    blocks = [block(chips)] + [block(chips // PIECES)] * PIECES
    tiles = jax.ShapeDtypeStruct((count, 8, LANES), jnp.float32)
    own, *send, scales = pl.pallas_call(
        lambda *refs: pair_kernel(chips, groups, *refs),
        name="quantize",
        grid=(count,),
        in_specs=[
            pl.BlockSpec(memory_space=pltpu.SMEM),
            pl.BlockSpec((1, 2 * chips * shard), lambda g: (0, g + start)),
            pl.BlockSpec(memory_space=pl.ANY),
        ],
        out_specs=[b for _, b in blocks] + [pl.BlockSpec((1, 8, LANES), lambda g: (g, 0, 0))],
        out_shape=[a for a, _ in blocks] + [tiles],
        scratch_shapes=[pltpu.VMEM((chips, 2 * groups, GROUP_ROWS, LANES), jnp.float32)],
        compiler_params=PARAMS_Q,
        cost_estimate=COST,
    )(place, grads, after)
    peer, peer_scales = jax.tree.map(lambda a: lax.ppermute(a, "core", [(0, 1), (1, 0)]), (send, scales))
    return own, peer, scales, peer_scales


def pair_sums(own, peer, scales, peer_scales, before, apart=False):
    chips, count, rows = own.shape[:3]
    half_spec = pl.BlockSpec((chips, 1, rows, LANES), lambda g: (0, g, 0, 0))
    piece_spec = pl.BlockSpec((chips // PIECES, 1, rows, LANES), lambda g: (0, g, 0, 0))
    tile_spec = pl.BlockSpec((1, 8, LANES), lambda g: (g, 0, 0))
    flag = jax.ShapeDtypeStruct((8, LANES), jnp.float32)
    whole = pl.BlockSpec((8, LANES), lambda g: (0, 0))
    length, copies = count * rows + AUX_ROWS, chips if apart else 1
    message = jax.ShapeDtypeStruct((length, LANES) if apart else (chips, length, LANES), jnp.bfloat16)
    *messages, flag = pl.pallas_call(
        lambda *refs: encode_kernel(chips, rows // GROUP_ROWS, count, apart, *refs),
        name="add_and_encode",
        grid=(count,),
        in_specs=[half_spec, tile_spec, tile_spec, whole] + [piece_spec] * PIECES,
        out_specs=[pl.BlockSpec(memory_space=pl.ANY)] * copies + [whole],
        out_shape=[message] * copies + [flag],
        scratch_shapes=[
            pltpu.VMEM((2, chips, rows, LANES), jnp.bfloat16),
            pltpu.VMEM((chips, AUX_ROWS, LANES), jnp.bfloat16),
            pltpu.VMEM((chips, 8, LANES), jnp.float32),
            pltpu.VMEM((8, LANES), jnp.float32),
            pltpu.SemaphoreType.DMA((2, copies)),
            pltpu.SemaphoreType.DMA((copies,)),
        ],
        compiler_params=PARAMS_C,
        cost_estimate=COST,
    )(own, scales, peer_scales, before, *peer)
    return messages, flag


def node_sums(received, count, chips, rows, earlier=None):
    groups = rows // GROUP_ROWS
    in_specs = [
        pl.BlockSpec((chips, rows, LANES), lambda g: (0, g, 0)),
        pl.BlockSpec((chips, AUX_ROWS, LANES), lambda g: (0, count * rows // AUX_ROWS, 0)),
    ]
    units = pltpu.VMEM((chips, 8, LANES), jnp.float32)
    if earlier is None:
        return pl.pallas_call(
            lambda *refs: decode_kernel(chips, groups, *refs),
            name="decode_and_requantize",
            grid=(count,),
            in_specs=in_specs,
            out_specs=pl.BlockSpec((1, rows, LANES), lambda g: (g, 0, 0)),
            out_shape=jax.ShapeDtypeStruct((count, rows, LANES), jnp.bfloat16),
            scratch_shapes=[units],
            compiler_params=PARAMS,
            cost_estimate=COST,
        )(received, received)
    replicas = count + sum(e.shape[0] for e in earlier)
    each = 2 if count % 2 == 0 else 1
    return pl.pallas_call(
        lambda *refs: last_decode_kernel(chips, groups, count, each, *refs),
        name="last_decode_and_requantize",
        grid=(count // each,),
        in_specs=[pl.BlockSpec((each * rows, LANES), lambda g: (g, 0))] * chips
        + [pl.BlockSpec((AUX_ROWS, LANES), lambda g: (count * rows // AUX_ROWS, 0))] * chips
        + [pl.BlockSpec(memory_space=pl.ANY)] * len(earlier),
        out_specs=pl.BlockSpec(memory_space=pl.ANY),
        out_shape=jax.ShapeDtypeStruct((replicas, rows, LANES), jnp.bfloat16),
        scratch_shapes=[
            pltpu.VMEM((2, each, rows, LANES), jnp.bfloat16),
            units,
            pltpu.SMEM((1,), jnp.int32),
            pltpu.SemaphoreType.DMA((2, each)),
            pltpu.SemaphoreType.DMA((replicas - count,)),
        ],
        compiler_params=PARAMS,
        cost_estimate=COST,
    )(*received, *received, *earlier)


def plain_sums(grads, after, replicas, nodes, shard):
    rows, groups = shard // LANES, shard // GROUP
    first = pl.pallas_call(
        lambda *refs: first_kernel(nodes, groups, *refs),
        name="plain_quantize",
        grid=(replicas,),
        in_specs=[
            pl.BlockSpec(memory_space=pltpu.SMEM),
            pl.BlockSpec((1, nodes * shard), lambda g: (0, g)),
        ],
        out_specs=pl.BlockSpec((nodes, 1, rows, LANES), lambda g: (0, g, 0, 0)),
        out_shape=jax.ShapeDtypeStruct((nodes, replicas, rows, LANES), jnp.bfloat16),
        scratch_shapes=[pltpu.VMEM((groups, GROUP_ROWS, LANES), jnp.float32)],
        compiler_params=PARAMS,
    )(after, grads)
    received = lax.all_to_all(first, ("chip", "core"), split_axis=0, concat_axis=0, tiled=True)
    partial = pl.pallas_call(
        lambda *refs: second_kernel(nodes, groups, *refs),
        name="plain_requantize",
        grid=(replicas,),
        in_specs=[pl.BlockSpec((nodes, 1, rows, LANES), lambda g: (0, g, 0, 0))],
        out_specs=pl.BlockSpec((1, rows, LANES), lambda g: (g, 0, 0)),
        out_shape=jax.ShapeDtypeStruct((replicas, rows, LANES), jnp.bfloat16),
        compiler_params=PARAMS,
    )(received)
    return lax.all_to_all(partial, GROUP_AXES, split_axis=0, concat_axis=0, tiled=True)


def update(owned, master, moment, second):
    replicas, rows = owned.shape[:2]
    state = jax.ShapeDtypeStruct((rows, LANES), jnp.float32)
    whole = pl.BlockSpec(memory_space=pltpu.VMEM)
    return pl.pallas_call(
        lambda *refs: update_kernel(replicas, rows // GROUP_ROWS, *refs),
        name="adamw_update",
        out_shape=(state, state, state, jax.ShapeDtypeStruct((1,), jnp.int32)),
        out_specs=(whole, whole, whole, pl.BlockSpec(memory_space=pltpu.SMEM)),
        scratch_shapes=[pltpu.VMEM((rows, LANES), jnp.float32)],
        compiler_params=PARAMS,
    )(owned, master, moment, second)


def body(grads, master, moment, second):
    replicas = lax.axis_size(GROUP_AXES)
    chips = lax.axis_size("chip")
    shard = master.shape[0]
    flag = jnp.zeros((8, LANES), jnp.float32)
    rows = shard // LANES
    partials, start = [], 0
    for count in PARTS:
        last = start + count == replicas
        ready = quantized(grads, flag, start, count, chips, shard, last)
        messages, flag = pair_sums(*ready, flag, last)
        if last:
            received = [
                lax.ppermute(m, "chip", [(c, other_chip(c, k)) for c in range(chips)]) if k else m
                for k, m in enumerate(messages)
            ]
        else:
            received = lax.all_to_all(messages[0], "chip", split_axis=0, concat_axis=0, tiled=True)
        partials.append(node_sums(received, count, chips, rows, partials if last else None))
        start += count
    owned = lax.all_to_all(partials[-1], GROUP_AXES[::-1], split_axis=0, concat_axis=0, tiled=True)
    state = [a.reshape(shard // LANES, LANES) for a in (master, moment, second)]

    def general(carry):
        *_, done = update(plain_sums(grads, carry[3], replicas, 2 * chips, shard), *state)
        return (*_, jnp.zeros_like(done))

    *outs, _ = lax.while_loop(lambda carry: carry[3][0] > 0, general, update(owned, *state))
    return tuple(a.reshape(shard) for a in outs)


def solution(mesh):
    nodes = mesh.devices.shape[1]
    axes = (*GROUP_AXES, "chip", "core")
    cores = Mesh(mesh.devices.reshape(*[2] * len(GROUP_AXES), nodes // 2, 2), axes)
    split = P(axes)
    in_specs = (P(axes, None), split, split, split)
    return jax.shard_map(
        body, mesh=cores, in_specs=in_specs, out_specs=(split, split, split), check_vma=False
    )
```
